256 devices in a mesh: seq: 64 (over z_hi, y, x, core), kv: 4 (over z_lo).
Axes of the slice: x: 4, y: 4, z: 8 (z_hi: 2, z_lo: 4; z = z_hi * 4 + z_lo), core: 2. Of those that a mesh axis runs over, the one named last changes fastest.
Arguments:
- queries: bfloat16 [32768, 4096], P('seq', 'kv'), may hold values from -8 to 8, as said below
- keys: bfloat16 [32768, 1024], P('seq', 'kv'), may hold values from -8 to 8, as said below
- values: bfloat16 [32768, 1024], P('seq', 'kv'), may hold values from -6 to 6
- kept_index: int32 [64, 32, 4], P('seq', 'kv'), may hold values from 0 to 3
- kept_count: int32 [64, 32], P('seq', 'kv'), may hold values from 3 to 4
- owner: int32 [64, 32, 4], P('seq', 'kv'), may hold values from 0 to 63, as said below
Outputs:
- attended: bfloat16 [32768, 4096], P('seq', 'kv')
- block_scores: float32 [32, 256], P('kv', 'seq')
- recv_keys: bfloat16 [64, 4, 64, 1, 128, 128], P('seq', 'kv')
- recv_values: bfloat16 [64, 4, 64, 1, 128, 128], P('seq', 'kv')
- recv_scores: bfloat16 [64, 4, 64, 1], P('seq', 'kv')
The draws below stay inside these ranges and needn't reach their ends.
Inputs may be any that keep to these rules, and one draw needn't show every extreme that they name: `queries`: entries of order one. `keys`: entries of order one. `kept_index`: a list may repeat a block. Entries c >= kept_count are padding and are not delivered. Within one shard and one lane no owner is named by more than 1 entries, valid or not; in each lane one owner is named by the first entry of the lane's first head in every shard.
All inputs are finite; a program needn't handle non-finite values.
Results may differ from the reference program's by a relative error of at most 0.0075.
Values may be sent and summed in bfloat16 or wider, within the bound.
No kernel may reach another device: no remote copies, remote signals or barrier semaphores. Data moves between devices by JAX's collectives and lax.ppermute only.
A program may use at most 128 MiB of HBM per device.

```python
import math
import jax
import jax.numpy as jnp
from jax import lax

QH = 32
KVH = 8
HD = 128
TOK_DEV = 512
CYCLE = 4
OBS = 64
BLOCK = 128
KEEP = 4
TOKENS = 32768
BLK_DEV = 4
NBLK = 256
CAP = 1
N_SEQ = 64
N_KV = 4


def shared_signs(key):
    picked = jax.random.bernoulli(jax.random.fold_in(key, 501), 0.5, (HD,))
    return jnp.where(picked, 1.0, -1.0).astype(jnp.float32)


def draw_queries(key, part):
    signs = shared_signs(key)
    key = jax.random.fold_in(key, 11)
    global_pos = jnp.arange(TOKENS, dtype=jnp.int32)
    base = jnp.clip(jax.random.normal(key, (TOKENS, QH, HD), jnp.float32), -6.0, 6.0)
    watching = (global_pos >= TOKENS - OBS).astype(jnp.float32)
    base = base + 0.5 * watching[:, None, None] * signs[None, None, :]
    return base.reshape(TOKENS, QH * HD).astype(jnp.bfloat16)


def draw_keys(key, part):
    signs = shared_signs(key)
    key = jax.random.fold_in(key, 23)
    global_pos = jnp.arange(TOKENS, dtype=jnp.int32)
    base = jnp.clip(jax.random.normal(key, (TOKENS, KVH, HD), jnp.float32), -6.0, 6.0)
    rising = 1.6 / (0.5 * math.sqrt(HD)) * global_pos.astype(jnp.float32) / TOKENS
    base = base + rising[:, None, None] * signs[None, None, :]
    return base.reshape(TOKENS, KVH * HD).astype(jnp.bfloat16)


def draw_owner(key, part):
    key = jax.random.fold_in(key, 31)
    per_lane = QH // N_KV * KEEP
    first_owner = jax.random.randint(jax.random.fold_in(key, 1), (N_KV,), 0, N_SEQ)
    seeds = jax.random.split(jax.random.fold_in(key, 2), N_SEQ * N_KV)

    def one_order(seed_key):
        return jax.random.permutation(seed_key, N_SEQ * CAP - 1)
    orders = jax.vmap(one_order)(seeds)[:, :per_lane - 1].astype(jnp.int32)
    seats = jnp.concatenate([jnp.zeros((N_SEQ * N_KV, 1), jnp.int32), orders + 1], axis=1)
    seats = seats.reshape(N_SEQ, N_KV, per_lane)
    owners = (first_owner[None, :, None] + seats // CAP) % N_SEQ
    return owners.reshape(N_SEQ, QH, KEEP).astype(jnp.int32)


def set_ends(drawn, stream_key, smallest, largest):
    place = [jax.random.randint(jax.random.fold_in(stream_key, axis), (), 0, length) for axis, length in enumerate(drawn.shape)]
    main_axis = drawn.shape.index(max(drawn.shape))
    next_to = place[:main_axis] + [(place[main_axis] + 1) % drawn.shape[main_axis]] + place[main_axis + 1:]
    return drawn.at[tuple(place)].set(smallest).at[tuple(next_to)].set(largest)


def shard_levels(stream_key, dims, cuts, low, high):
    gain, own = 1.0, jax.random.fold_in(stream_key, 6)
    for position, parts in cuts:
        draws = jnp.exp(jax.random.uniform(jax.random.fold_in(own, position), (parts,), jnp.float32, low / len(cuts), high / len(cuts)))
        gain = gain * jnp.repeat(draws, dims[position] // parts).reshape([-1 if axis == position else 1 for axis in range(len(dims))])
    return gain


def normal_values(stream_key, shape, deviation, reach, pieces=(), kind=jnp.bfloat16):
    factor_of = shard_levels(stream_key, shape, pieces, -0.22, 0.18) if pieces else 1.0
    result = jax.random.normal(stream_key, shape, jnp.float32) * deviation * factor_of
    return jnp.minimum(jnp.maximum(result, -reach), reach).astype(kind)


def setup_inputs(seed: int = 0) -> dict:
    arg_keys = jax.random.split(jax.random.key(seed), 7)
    return {
        "queries": draw_queries(jax.random.fold_in(arg_keys[6], 71), 0),
        "keys": draw_keys(jax.random.fold_in(arg_keys[6], 71), 0),
        "values": normal_values(arg_keys[2], (TOKENS, KVH * HD), 1.0, 6.0, ((0, 64), (1, 4))),
        "kept_index": set_ends(jax.random.randint(arg_keys[3], (N_SEQ, QH, KEEP), 0, BLK_DEV), jax.random.fold_in(arg_keys[3], 1), 0, BLK_DEV - 1).astype(jnp.int32),
        "kept_count": set_ends(jax.random.randint(arg_keys[4], (N_SEQ, QH), KEEP - 1, KEEP + 1), jax.random.fold_in(arg_keys[4], 1), KEEP - 1, KEEP).astype(jnp.int32),
        "owner": draw_owner(jax.random.fold_in(arg_keys[6], 71), 0),
    }


def reference(queries, keys, values, kept_index, kept_count, owner):
    group = QH // KVH
    scale = 1.0 / math.sqrt(HD)
    span = CYCLE * TOK_DEV
    query_shards = queries.reshape(N_SEQ, TOK_DEV, KVH, group, HD)
    padding = jnp.zeros(((CYCLE - 1) * TOK_DEV, KVH * HD), jnp.bfloat16)
    keys_padded = jnp.concatenate([padding, keys], axis=0)
    values_padded = jnp.concatenate([padding, values], axis=0)

    def shard_attention(shard):
        query_block = lax.dynamic_index_in_dim(query_shards, shard, 0, keepdims=False).astype(jnp.float32)
        start = (shard * TOK_DEV).astype(jnp.int32)
        key_block = lax.dynamic_slice_in_dim(keys_padded, start, span, 0).reshape(span, KVH, HD).astype(jnp.float32)
        value_block = lax.dynamic_slice_in_dim(values_padded, start, span, 0).reshape(span, KVH, HD).astype(jnp.float32)
        score = jnp.einsum('tkgd,jkd->kgtj', query_block, key_block) * scale
        query_pos = shard * TOK_DEV + jnp.arange(TOK_DEV, dtype=jnp.int32)
        key_pos = (shard - (CYCLE - 1)) * TOK_DEV + jnp.arange(span, dtype=jnp.int32)
        seen = (key_pos[None, :] <= query_pos[:, None]) & (key_pos[None, :] >= 0)
        score = jnp.where(seen, score, -jnp.inf)
        peak = lax.optimization_barrier(jnp.max(score, axis=-1, keepdims=True))
        weights = jnp.exp(score - peak)
        total = lax.optimization_barrier(jnp.sum(weights, axis=-1))
        weights_low = lax.optimization_barrier(weights.astype(jnp.bfloat16)).astype(jnp.float32)
        mixed = jnp.einsum('kgtj,jkd->tkgd', weights_low, value_block)
        mixed = mixed / jnp.transpose(total, (2, 0, 1))[..., None]
        return mixed.reshape(TOK_DEV, QH * HD).astype(jnp.bfloat16)
    attended = lax.map(shard_attention, jnp.arange(N_SEQ, dtype=jnp.int32)).reshape(TOKENS, QH * HD)
    observers = queries[TOKENS - OBS:].reshape(OBS, KVH, group, HD).astype(jnp.float32)
    key_heads = jnp.transpose(keys.reshape(TOKENS, KVH, HD), (1, 0, 2))
    obs_pos = TOKENS - OBS + jnp.arange(OBS, dtype=jnp.int32)
    all_pos = jnp.arange(TOKENS, dtype=jnp.int32)
    visible = all_pos[None, :] <= obs_pos[:, None]

    def head_scores(operands):
        query_head, key_head = operands
        score = jnp.einsum('ogd,jd->goj', query_head, key_head.astype(jnp.float32)) * scale
        score = jnp.where(visible[None], score, -jnp.inf)
        peak = lax.optimization_barrier(jnp.max(score, axis=-1, keepdims=True))
        expo = jnp.exp(score - peak)
        prob = expo / lax.optimization_barrier(jnp.sum(expo, axis=-1, keepdims=True))
        per_key = lax.optimization_barrier(jnp.sum(prob, axis=1))
        return lax.optimization_barrier(jnp.sum(per_key.reshape(group, NBLK, BLOCK), axis=-1)) * (NBLK / OBS)
    block_scores = lax.map(head_scores, (jnp.transpose(observers, (1, 0, 2, 3)), key_heads)).reshape(QH, NBLK)
    lane_heads = QH // N_KV
    entries = lane_heads * KEEP
    entry_ids = jnp.arange(entries, dtype=jnp.int32)
    entry_head = entry_ids // KEEP
    entry_slot = entry_ids % KEEP
    owners = owner.reshape(N_SEQ, N_KV, entries)
    picks = kept_index.reshape(N_SEQ, N_KV, entries)
    counts = kept_count.reshape(N_SEQ, N_KV, lane_heads)[:, :, entry_head]
    valid = entry_slot[None, None, :] < counts
    earlier = (owners[..., :, None] == owners[..., None, :]) & valid[..., None, :] & (entry_ids[None, :] < entry_ids[:, None])
    slot = lax.optimization_barrier(jnp.sum(earlier.astype(jnp.int32), axis=-1))
    lane_ids = jnp.arange(N_KV, dtype=jnp.int32)
    shard_ids = jnp.arange(N_SEQ, dtype=jnp.int32)
    head_global = lane_ids[:, None] * lane_heads + entry_head[None, :]
    kv_global = head_global // group
    block_global = shard_ids[:, None, None] * BLK_DEV + picks
    key_blocks = keys.reshape(NBLK, BLOCK, KVH, HD)
    value_blocks = values.reshape(NBLK, BLOCK, KVH, HD)
    kv_full = jnp.broadcast_to(kv_global[None], (N_SEQ, N_KV, entries))
    sent_keys = key_blocks[block_global, :, kv_full, :]
    sent_values = value_blocks[block_global, :, kv_full, :]
    sent_scores = block_scores[jnp.broadcast_to(head_global[None], (N_SEQ, N_KV, entries)), block_global]
    target = jnp.where(valid, owners, N_SEQ)
    lane_full = jnp.broadcast_to(lane_ids[None, :, None], (N_SEQ, N_KV, entries))
    shard_full = jnp.broadcast_to(shard_ids[:, None, None], (N_SEQ, N_KV, entries))
    recv_keys = jnp.zeros((N_SEQ, N_KV, N_SEQ, CAP, BLOCK, HD), jnp.bfloat16).at[target, lane_full, shard_full, slot].set(sent_keys, mode='drop')
    recv_values = jnp.zeros((N_SEQ, N_KV, N_SEQ, CAP, BLOCK, HD), jnp.bfloat16).at[target, lane_full, shard_full, slot].set(sent_values, mode='drop')
    recv_scores = jnp.zeros((N_SEQ, N_KV, N_SEQ, CAP), jnp.bfloat16).at[target, lane_full, shard_full, slot].set(sent_scores.astype(jnp.bfloat16), mode='drop')
    return (attended, block_scores, recv_keys, recv_values, recv_scores)
```

```python
import math

import jax
import jax.numpy as jnp
from jax import lax
from jax.experimental import pallas as pl
from jax.experimental.pallas import tpu as pltpu
from jax.sharding import Mesh, PartitionSpec as P

HD = 128
CYCLE = 4
OBS = 64
BLOCK = 128
SHARD = 512
HEADS = 8
KVS = 2
GROUP = 4
KEEP = 4
BLKS = 4
NSEQ = 64
HALF = 32
SEQ = ("zh", "y", "x", "c")
PLANE = ("y", "x", "c")
LOG2E = 1.4426950408889634
COEF = LOG2E / math.sqrt(HD)
SCALE = 1.0 / math.sqrt(HD)
BIG = 1e30
NT = (((1,), (1,)), ((), ()))


def f32dot(a, b, dims):
    return lax.dot_general(a, b, dims, preferred_element_type=jnp.float32)


def attend_kernel(pos_ref, q_ref, k0, k1, k2, k3, v0, v1, v2, v3, o_ref):
    pos = pos_ref[0]
    half = SHARD // 2
    ones = jnp.ones((SHARD, HD), jnp.bfloat16)
    vext = [jnp.concatenate([v[...], ones], axis=1) for v in (v0, v1, v2, v3)]
    row = lax.broadcasted_iota(jnp.int32, (half, half), 0)
    col = lax.broadcasted_iota(jnp.int32, (half, half), 1)
    causal = col <= row
    for tile in range(2):
        q = q_ref[tile * half : (tile + 1) * half, :]
        diag = f32dot(q, k0[tile * half : (tile + 1) * half, :], NT)
        diag = jnp.where(causal, diag, -BIG)
        peak = jnp.max(diag, axis=1, keepdims=True)
        full = []
        if tile == 1:
            own = f32dot(q, k0[:half, :], NT)
            peak = jnp.maximum(peak, jnp.max(own, axis=1, keepdims=True))
            full.append(own)
        past = [f32dot(q, k[...], NT) for k in (k1, k2, k3)]
        for distance, score in enumerate(past, 1):
            here = jnp.max(score, axis=1, keepdims=True)
            peak = jnp.where(pos >= distance, jnp.maximum(peak, here), peak)
        shift = peak * COEF
        weight = jnp.exp2(diag * COEF - shift).astype(jnp.bfloat16)
        acc = f32dot(weight, vext[0][tile * half : (tile + 1) * half], (((1,), (0,)), ((), ())))
        if tile == 1:
            weight = jnp.exp2(full[0] * COEF - shift).astype(jnp.bfloat16)
            acc += f32dot(weight, vext[0][:half], (((1,), (0,)), ((), ())))
        for distance, score in enumerate(past, 1):
            lift = jnp.where(pos >= distance, shift, BIG)
            weight = jnp.exp2(score * COEF - lift).astype(jnp.bfloat16)
            acc += f32dot(weight, vext[distance], (((1,), (0,)), ((), ())))
        mixed = acc[:, :HD] / acc[:, HD:]
        o_ref[tile * half : (tile + 1) * half, :] = mixed.astype(jnp.bfloat16)


def attend(position, queries, ks, vs):
    kv_spec = pl.BlockSpec((SHARD, HD), lambda h: (0, h // GROUP))
    return pl.pallas_call(
        attend_kernel,
        grid=(HEADS,),
        out_shape=jax.ShapeDtypeStruct((SHARD, HEADS * HD), jnp.bfloat16),
        in_specs=[
            pl.BlockSpec(memory_space=pltpu.SMEM),
            pl.BlockSpec((SHARD, HD), lambda h: (0, h)),
        ]
        + [kv_spec] * 8,
        out_specs=pl.BlockSpec((SHARD, HD), lambda h: (0, h)),
        compiler_params=pltpu.CompilerParams(vmem_limit_bytes=32 * 1024 * 1024),
        cost_estimate=pl.CostEstimate(
            flops=HEADS * SHARD * SHARD * 4 * HD * 4,
            bytes_accessed=4 * 1024 * 1024,
            transcendentals=HEADS * SHARD * SHARD * 4,
        ),
        name="attend",
    )(position, queries, *ks, *vs)


def pack_kernel(base_ref, meta_ref, k_ref, v_ref, out_ref):
    base = base_ref[0]
    out_ref[...] = jnp.zeros_like(out_ref)
    for head in range(HEADS):
        lo = (head // GROUP) * HD
        for c in range(KEEP):
            seat = meta_ref[c, head] - base
            rows = pl.ds(pl.multiple_of(meta_ref[KEEP + c, head] * BLOCK, BLOCK), BLOCK)

            @pl.when((seat >= 0) & (seat < HALF))
            def _():
                out_ref[seat, 0] = k_ref[rows, lo : lo + HD]
                out_ref[seat, 1] = v_ref[rows, lo : lo + HD]


def pack(base, meta, keys, values):
    return pl.pallas_call(
        pack_kernel,
        out_shape=jax.ShapeDtypeStruct((HALF, 2, BLOCK, HD), jnp.bfloat16),
        in_specs=[
            pl.BlockSpec(memory_space=pltpu.SMEM),
            pl.BlockSpec(memory_space=pltpu.SMEM),
            pl.BlockSpec(memory_space=pltpu.VMEM),
            pl.BlockSpec(memory_space=pltpu.VMEM),
        ],
        out_specs=pl.BlockSpec(memory_space=pltpu.VMEM),
        compiler_params=pltpu.CompilerParams(vmem_limit_bytes=16 * 1024 * 1024),
        cost_estimate=pl.CostEstimate(flops=0, bytes_accessed=5 * 1024 * 1024, transcendentals=0),
        name="pack",
    )(base, meta, keys, values)


def observe_kernel(pos_ref, meta_ref, q_ref, k_ref, msg_ref, frac_ref, level_ref):
    pos = pos_ref[0]
    levels = []
    fracs = [[] for _ in range(BLKS)]
    for kv in range(KVS):
        rows = [
            q_ref[:, (kv * GROUP + g) * HD : (kv * GROUP + g + 1) * HD] for g in range(GROUP)
        ]
        stacked = jnp.concatenate(rows, axis=0)
        score = f32dot(k_ref[:, kv * HD : (kv + 1) * HD], stacked, NT) * SCALE
        key = lax.broadcasted_iota(jnp.int32, score.shape, 0)
        lane = lax.broadcasted_iota(jnp.int32, score.shape, 1)
        limit = (NSEQ - pos) * SHARD - OBS + lax.rem(lane, OBS)
        score = jnp.where(key <= limit, score, -jnp.inf)
        peak = jnp.max(score, axis=0, keepdims=True)
        expo = jnp.exp(score - peak)
        sums = [
            jnp.sum(expo[b * BLOCK : (b + 1) * BLOCK], axis=0, keepdims=True) for b in range(BLKS)
        ]
        mass = (sums[0] + sums[1]) + (sums[2] + sums[3])
        level = peak + jnp.log(mass)
        for side in range(2):
            cut = slice(side * 128, (side + 1) * 128)
            levels.append(level[:, cut])
            for b in range(BLKS):
                fracs[b].append((sums[b] / mass)[:, cut])
    level4 = jnp.concatenate(levels, axis=0)
    level_ref[...] = level4
    for b in range(BLKS):
        frac_ref[b] = jnp.concatenate(fracs[b], axis=0)
    blank = jnp.concatenate([level4, jnp.zeros_like(level4)], axis=0)
    msg_ref[...] = jnp.broadcast_to(blank[None], msg_ref.shape)
    which = lax.broadcasted_iota(jnp.int32, (4, 128), 0) * 2 + (
        lax.broadcasted_iota(jnp.int32, (4, 128), 1) // OBS
    )
    for head in range(HEADS):
        for c in range(KEEP):
            target = meta_ref[c, head]
            unit = meta_ref[KEEP + c, head]

            @pl.when(target >= 0)
            def _():
                msg_ref[target, 4:8, :] = jnp.where(which == head, frac_ref[unit], 0.0)


def observe(position, meta, observers, keys):
    smem = pl.BlockSpec(memory_space=pltpu.SMEM)
    vmem = pl.BlockSpec(memory_space=pltpu.VMEM)
    return pl.pallas_call(
        observe_kernel,
        out_shape=(
            jax.ShapeDtypeStruct((NSEQ, 8, 128), jnp.float32),
            jax.ShapeDtypeStruct((BLKS, 4, 128), jnp.float32),
            jax.ShapeDtypeStruct((4, 128), jnp.float32),
        ),
        in_specs=[smem, smem, vmem, vmem],
        out_specs=(vmem, vmem, vmem),
        compiler_params=pltpu.CompilerParams(vmem_limit_bytes=16 * 1024 * 1024),
        name="observe",
    )(position, meta, observers, keys)


def finish_kernel(got_ref, frac_ref, level_ref, recv_ref, block_ref):
    level = got_ref[:, 0:4, :]
    top = jnp.max(level, axis=0)
    total = top + jnp.log(jnp.sum(jnp.exp(level - top[None]), axis=0))
    share = got_ref[:, 4:8, :] * jnp.exp(level - total[None])
    factor = BLKS * NSEQ / OBS
    recv = jnp.sum(jnp.sum(share, axis=1), axis=1, keepdims=True) * factor
    recv_ref[...] = recv.astype(jnp.bfloat16)
    own = jnp.exp(level_ref[...] - total)
    side = lax.broadcasted_iota(jnp.int32, (HEADS, 128), 1) // OBS
    odd = lax.rem(lax.broadcasted_iota(jnp.int32, (HEADS, 128), 0), 2)
    columns = []
    for b in range(BLKS):
        part = frac_ref[b] * own
        twice = jnp.concatenate([part[h // 2 : h // 2 + 1] for h in range(HEADS)], axis=0)
        picked = jnp.where(side == odd, twice, 0.0)
        columns.append(jnp.sum(picked, axis=1, keepdims=True))
    block_ref[...] = jnp.concatenate(columns, axis=1) * factor


def finish(got, frac, level):
    vmem = pl.BlockSpec(memory_space=pltpu.VMEM)
    return pl.pallas_call(
        finish_kernel,
        out_shape=(
            jax.ShapeDtypeStruct((NSEQ, 1), jnp.bfloat16),
            jax.ShapeDtypeStruct((HEADS, BLKS), jnp.float32),
        ),
        in_specs=[vmem] * 3,
        out_specs=(vmem, vmem),
        name="finish",
    )(got, frac, level)


def place_kernel(half_ref, got_ref, *refs):
    key_ref, value_ref, sems = refs[-3:]
    half = half_ref[0]
    one = pltpu.make_async_copy(got_ref.at[:, 0], key_ref.at[pl.ds(half * HALF, HALF)], sems.at[0])
    two = pltpu.make_async_copy(
        got_ref.at[:, 1], value_ref.at[pl.ds(half * HALF, HALF)], sems.at[1]
    )
    one.start()
    two.start()
    one.wait()
    two.wait()


def place(half, got, earlier=None):
    any_ = pl.BlockSpec(memory_space=pl.ANY)
    shape = jax.ShapeDtypeStruct((NSEQ, BLOCK, HD), jnp.bfloat16)
    operands = (half, got) if earlier is None else (half, got) + tuple(earlier)
    return pl.pallas_call(
        place_kernel,
        out_shape=(shape, shape),
        in_specs=[pl.BlockSpec(memory_space=pltpu.SMEM)] + [any_] * (len(operands) - 1),
        out_specs=(any_, any_),
        scratch_shapes=[pltpu.SemaphoreType.DMA((2,))],
        input_output_aliases={} if earlier is None else {2: 0, 3: 1},
        cost_estimate=pl.CostEstimate(flops=0, bytes_accessed=4 * 1024 * 1024, transcendentals=0),
        name="place",
    )(*operands)


def spread(tail):
    me = lax.axis_index(SEQ)
    held = jnp.where(me == NSEQ - 1, tail, jnp.zeros_like(tail))

    def index(zh, y, x, c):
        return ((zh * 4 + y) * 4 + x) * 2 + c

    steps = (
        [[(index(1, 3, 3, 1), index(1, y, 3, 1))] for y in range(3)],
        [[(index(1, y, 3, 1), index(1, y, x, 1)) for y in range(4)] for x in range(3)],
        [
            [(index(1, y, x, 1), index(zh, y, x, c)) for y in range(4) for x in range(4)]
            for zh, c in ((0, 1), (0, 0), (1, 0))
        ],
    )
    for step in steps:
        came = [lax.ppermute(held, SEQ, pairs) for pairs in step]
        held = held + ((came[0] + came[1]) + came[2])
    return held


def shards(queries, keys, values, kept_index, kept_count, owner):
    position = lax.axis_index(SEQ)
    zh = lax.axis_index("zh")
    pos = position.reshape(1).astype(jnp.int32)
    base = (zh * HALF).reshape(1).astype(jnp.int32)
    slot_ids = jnp.arange(KEEP, dtype=jnp.int32)[:, None]
    owners = jnp.transpose(owner, (0, 2, 1))[0]
    picks = jnp.transpose(kept_index, (0, 2, 1))[0]
    meta = jnp.concatenate([jnp.where(slot_ids < kept_count, owners, -1), picks], axis=0)

    observers = spread(queries[SHARD - OBS :])

    swap = [(0, 1), (1, 0)]
    other_meta = lax.ppermute(meta, "zh", swap)
    other_keys = lax.ppermute(keys, "zh", swap)
    other_values = lax.ppermute(values, "zh", swap)

    def exchange(packed):
        return lax.all_to_all(packed, PLANE, split_axis=0, concat_axis=0, tiled=True)

    near = exchange(pack(base, meta, keys, values))

    pairs = [(i, i + 1) for i in range(NSEQ - 1)]
    ks, vs = [keys], [values]
    for _ in range(1, CYCLE):
        ks.append(lax.ppermute(ks[-1], SEQ, pairs))
        vs.append(lax.ppermute(vs[-1], SEQ, pairs))

    msg, frac, level = observe(pos, meta, observers, keys)
    got = lax.all_to_all(msg, SEQ, split_axis=0, concat_axis=0, tiled=True)
    attended = attend(pos, queries, ks, vs)
    recv_scores, scores_here = finish(got, frac, level)

    far = exchange(pack(base, other_meta, other_keys, other_values))
    first = place(zh.reshape(1).astype(jnp.int32), near)
    recv_keys, recv_values = place((1 - zh).reshape(1).astype(jnp.int32), far, first)
    return (
        attended,
        scores_here,
        recv_keys.reshape(1, 1, NSEQ, 1, BLOCK, HD),
        recv_values.reshape(1, 1, NSEQ, 1, BLOCK, HD),
        recv_scores.reshape(1, 1, NSEQ, 1),
    )


def solution(mesh):
    fine = Mesh(mesh.devices.reshape(2, 4, 4, 2, 4), SEQ + ("kv",))
    placed = (
        P(SEQ, "kv"),
        P(SEQ, "kv"),
        P(SEQ, "kv"),
        P(SEQ, "kv", None),
        P(SEQ, "kv"),
        P(SEQ, "kv", None),
    )
    return jax.shard_map(
        shards,
        mesh=fine,
        in_specs=placed,
        out_specs=(
            P(SEQ, "kv"),
            P("kv", SEQ),
            P(SEQ, "kv", None, None, None, None),
            P(SEQ, "kv", None, None, None, None),
            P(SEQ, "kv", None, None),
        ),
        check_vma=False,
    )
```

```python
import functools
import math

import jax
import jax.numpy as jnp
from jax import lax
from jax.experimental import pallas as pl
from jax.experimental.pallas import tpu as pltpu
from jax.sharding import Mesh, PartitionSpec as P

HD = 128
CYCLE = 4
OBS = 64
BLOCK = 128
SHARD = 512
HEADS = 8
KVS = 2
GROUP = 4
KEEP = 4
BLKS = 4
NSEQ = 64
HALF = 32
SEQ = ("zh", "y", "x", "c")
PLANE = ("y", "x", "c")
LOG2E = 1.4426950408889634
COEF = LOG2E / math.sqrt(HD)
SCALE = 1.0 / math.sqrt(HD)
BIG = 1e30
NT = (((1,), (1,)), ((), ()))


def f32dot(a, b, dims):
    return lax.dot_general(a, b, dims, preferred_element_type=jnp.float32)


def attend_kernel(pos_ref, q_ref, k0, v0, k1, v1, k2, v2, k3, v3, o_ref):
    pos = pos_ref[0]
    half = SHARD // 2
    ones = jnp.ones((SHARD, HD), jnp.bfloat16)
    vext = [jnp.concatenate([v[...], ones], axis=1) for v in (v0, v1, v2, v3)]
    row = lax.broadcasted_iota(jnp.int32, (half, half), 0)
    col = lax.broadcasted_iota(jnp.int32, (half, half), 1)
    causal = col <= row
    for tile in range(2):
        q = q_ref[tile * half : (tile + 1) * half, :]
        diag = f32dot(q, k0[tile * half : (tile + 1) * half, :], NT)
        diag = jnp.where(causal, diag, -BIG)
        peak = jnp.max(diag, axis=1, keepdims=True)
        full = []
        if tile == 1:
            own = f32dot(q, k0[:half, :], NT)
            peak = jnp.maximum(peak, jnp.max(own, axis=1, keepdims=True))
            full.append(own)
        past = [f32dot(q, k[...], NT) for k in (k1, k2, k3)]
        for distance, score in enumerate(past, 1):
            here = jnp.max(score, axis=1, keepdims=True)
            peak = jnp.where(pos >= distance, jnp.maximum(peak, here), peak)
        shift = peak * COEF
        weight = jnp.exp2(diag * COEF - shift).astype(jnp.bfloat16)
        acc = f32dot(weight, vext[0][tile * half : (tile + 1) * half], (((1,), (0,)), ((), ())))
        if tile == 1:
            weight = jnp.exp2(full[0] * COEF - shift).astype(jnp.bfloat16)
            acc += f32dot(weight, vext[0][:half], (((1,), (0,)), ((), ())))
        for distance, score in enumerate(past, 1):
            lift = jnp.where(pos >= distance, shift, BIG)
            weight = jnp.exp2(score * COEF - lift).astype(jnp.bfloat16)
            acc += f32dot(weight, vext[distance], (((1,), (0,)), ((), ())))
        mixed = acc[:, :HD] / acc[:, HD:]
        o_ref[tile * half : (tile + 1) * half, :] = mixed.astype(jnp.bfloat16)


def attend(position, queries, pairs):
    key_spec = pl.BlockSpec((SHARD, HD), lambda h: (0, h // GROUP))
    value_spec = pl.BlockSpec((SHARD, HD), lambda h: (1, h // GROUP))
    return pl.pallas_call(
        attend_kernel,
        grid=(HEADS,),
        out_shape=jax.ShapeDtypeStruct((SHARD, HEADS * HD), jnp.bfloat16),
        in_specs=[
            pl.BlockSpec(memory_space=pltpu.SMEM),
            pl.BlockSpec((SHARD, HD), lambda h: (0, h)),
        ]
        + [key_spec, value_spec] * CYCLE,
        out_specs=pl.BlockSpec((SHARD, HD), lambda h: (0, h)),
        compiler_params=pltpu.CompilerParams(vmem_limit_bytes=32 * 1024 * 1024),
        cost_estimate=pl.CostEstimate(
            flops=HEADS * SHARD * SHARD * 4 * HD * 4,
            bytes_accessed=4 * 1024 * 1024,
            transcendentals=HEADS * SHARD * SHARD * 4,
        ),
        name="attend",
    )(position, queries, *[pair for pair in pairs for _ in range(2)])


SMEM = pl.BlockSpec(memory_space=pltpu.SMEM)
VMEM = pl.BlockSpec(memory_space=pltpu.VMEM)
ANY = pl.BlockSpec(memory_space=pl.ANY)


def seats(base, meta_ref, put):
    for head in range(HEADS):
        for c in range(KEEP):
            seat = meta_ref[c, head] - base
            unit = meta_ref[KEEP + c, head]
            pl.when((seat >= 0) & (seat < HALF))(functools.partial(put, seat, unit, head))


def block_rows(unit, start):
    return pl.ds(pl.multiple_of(unit * BLOCK + start, BLOCK), BLOCK)


def near_kernel(base_ref, meta_ref, k_ref, v_ref, out_ref, pair_ref):
    pair_ref[:SHARD] = k_ref[...]
    pair_ref[SHARD:] = v_ref[...]
    out_ref[...] = jnp.zeros_like(out_ref)

    def put(seat, unit, head):
        cols = slice((head // GROUP) * HD, (head // GROUP + 1) * HD)
        out_ref[seat, :BLOCK] = k_ref[block_rows(unit, 0), cols]
        out_ref[seat, BLOCK:] = v_ref[block_rows(unit, 0), cols]

    seats(base_ref[0], meta_ref, put)


def pack_near(base, meta, keys, values):
    return pl.pallas_call(
        near_kernel,
        out_shape=(
            jax.ShapeDtypeStruct((HALF, 2 * BLOCK, HD), jnp.bfloat16),
            jax.ShapeDtypeStruct((2 * SHARD, KVS * HD), jnp.bfloat16),
        ),
        in_specs=[SMEM, SMEM, VMEM, VMEM],
        out_specs=(VMEM, VMEM),
        compiler_params=pltpu.CompilerParams(vmem_limit_bytes=16 * 1024 * 1024),
        cost_estimate=pl.CostEstimate(flops=0, bytes_accessed=3 * 1024 * 1024, transcendentals=0),
        name="pack_near",
    )(base, meta, keys, values)


def terms(value, count):
    parts = []
    for _ in range(count):
        part = value.astype(jnp.bfloat16)
        parts.append(part)
        value = value - part.astype(jnp.float32)
    return parts


def far_kernel(
    base_ref, meta_ref, other_meta_ref, pair_ref, stats_ref, other_ref, out_ref, tile_ref
):
    level, other_level = stats_ref[0:4], other_ref[0:4]
    top = jnp.maximum(level, other_level)
    both = top + jnp.log(jnp.exp(level - top) + jnp.exp(other_level - top))
    part, other_part = jnp.exp(level - both), jnp.exp(other_level - both)
    blank = jnp.zeros((4, 128), jnp.float32)
    as_rows = lambda pieces: jnp.concatenate([p.astype(jnp.float32) for p in pieces], axis=0)
    for b in range(BLKS):
        rows = slice(4 + 4 * b, 8 + 4 * b)
        tile_ref[0, b] = as_rows(terms(stats_ref[rows] * part, 2) + [blank, blank])
        tile_ref[1, b] = as_rows([blank, blank] + terms(other_ref[rows] * other_part, 2))
    out_ref[:, : 2 * BLOCK, :] = jnp.zeros((HALF, 2 * BLOCK, HD), jnp.bfloat16)
    lead = as_rows(terms(both, 3) + [blank]).astype(jnp.bfloat16)
    out_ref[:, 2 * BLOCK : 2 * BLOCK + 16, :] = jnp.broadcast_to(lead[None], (HALF, 16, HD))
    out_ref[:, 2 * BLOCK + 16 :, :] = jnp.zeros((HALF, 16, HD), jnp.bfloat16)
    row = lax.broadcasted_iota(jnp.int32, (16, 128), 0)
    lane = lax.broadcasted_iota(jnp.int32, (16, 128), 1)
    which = lax.rem(row, 4) * 2 + lane // OBS
    tail = slice(2 * BLOCK + 16, 2 * BLOCK + 32)

    def add_score(source, seat, unit, head):
        picked = jnp.where(which == head, tile_ref[source, unit], 0.0).astype(jnp.bfloat16)
        out_ref[seat, tail] = out_ref[seat, tail] + picked

    def put(seat, unit, head):
        cols = slice((head // GROUP) * HD, (head // GROUP + 1) * HD)
        out_ref[seat, :BLOCK] = pair_ref[block_rows(unit, 0), cols]
        out_ref[seat, BLOCK : 2 * BLOCK] = pair_ref[block_rows(unit, SHARD), cols]
        add_score(1, seat, unit, head)

    seats(base_ref[0], meta_ref, functools.partial(add_score, 0))
    seats(base_ref[0], other_meta_ref, put)


def pack_far(base, meta, other_meta, other_pair, stats, other_stats):
    return pl.pallas_call(
        far_kernel,
        out_shape=jax.ShapeDtypeStruct((HALF, 2 * BLOCK + 32, HD), jnp.bfloat16),
        in_specs=[SMEM, SMEM, SMEM, VMEM, VMEM, VMEM],
        out_specs=VMEM,
        scratch_shapes=[pltpu.VMEM((2, BLKS, 16, 128), jnp.float32)],
        compiler_params=pltpu.CompilerParams(vmem_limit_bytes=16 * 1024 * 1024),
        cost_estimate=pl.CostEstimate(flops=0, bytes_accessed=3 * 1024 * 1024, transcendentals=0),
        name="pack_far",
    )(base, meta, other_meta, other_pair, stats, other_stats)


def observe_kernel(pos_ref, q_ref, k_ref, stats_ref):
    pos = pos_ref[0]
    rows = [[] for _ in range(1 + BLKS)]
    for kv in range(KVS):
        heads = [
            q_ref[:, (kv * GROUP + g) * HD : (kv * GROUP + g + 1) * HD] for g in range(GROUP)
        ]
        stacked = jnp.concatenate(heads, axis=0)
        score = f32dot(k_ref[:, kv * HD : (kv + 1) * HD], stacked, NT) * SCALE
        key = lax.broadcasted_iota(jnp.int32, score.shape, 0)
        lane = lax.broadcasted_iota(jnp.int32, score.shape, 1)
        limit = (NSEQ - pos) * SHARD - OBS + lax.rem(lane, OBS)
        score = jnp.where(key <= limit, score, -jnp.inf)
        peak = jnp.max(score, axis=0, keepdims=True)
        expo = jnp.exp(score - peak)
        sums = [
            jnp.sum(expo[b * BLOCK : (b + 1) * BLOCK], axis=0, keepdims=True) for b in range(BLKS)
        ]
        mass = (sums[0] + sums[1]) + (sums[2] + sums[3])
        level = peak + jnp.log(mass)
        for side in range(2):
            cut = slice(side * 128, (side + 1) * 128)
            rows[0].append(level[:, cut])
            for b in range(BLKS):
                rows[1 + b].append((sums[b] / mass)[:, cut])
    for place_, pieces in enumerate(rows):
        stats_ref[4 * place_ : 4 * place_ + 4] = jnp.concatenate(pieces, axis=0)
    stats_ref[20:24] = jnp.zeros((4, 128), jnp.float32)


def observe(position, observers, keys):
    return pl.pallas_call(
        observe_kernel,
        out_shape=jax.ShapeDtypeStruct((24, 128), jnp.float32),
        in_specs=[SMEM, VMEM, VMEM],
        out_specs=VMEM,
        compiler_params=pltpu.CompilerParams(vmem_limit_bytes=16 * 1024 * 1024),
        name="observe",
    )(position, observers, keys)


CHUNK = 4


def place_kernel(half_ref, got_ref, key_ref, value_ref):
    key_ref[...] = got_ref[:, :BLOCK]
    value_ref[...] = got_ref[:, BLOCK : 2 * BLOCK]


def place_near(half, got):
    shape = jax.ShapeDtypeStruct((NSEQ, BLOCK, HD), jnp.bfloat16)
    out_spec = pl.BlockSpec((CHUNK, BLOCK, HD), lambda i, half: (half[0] * (HALF // CHUNK) + i, 0, 0))
    return pl.pallas_call(
        place_kernel,
        out_shape=(shape, shape),
        grid_spec=pltpu.PrefetchScalarGridSpec(
            num_scalar_prefetch=1,
            grid=(HALF // CHUNK,),
            in_specs=[pl.BlockSpec((CHUNK, 2 * BLOCK, HD), lambda i, half: (i, 0, 0))],
            out_specs=(out_spec, out_spec),
        ),
        cost_estimate=pl.CostEstimate(flops=0, bytes_accessed=4 * 1024 * 1024, transcendentals=0),
        name="place_near",
    )(half, got)


def last_kernel(
    half_ref, got_ref, mail_ref, stats_ref, _k, _v, key_ref, value_ref, recv_ref, block_ref
):
    key_ref[...] = got_ref[:, :BLOCK]
    value_ref[...] = got_ref[:, BLOCK : 2 * BLOCK]

    @pl.when(pl.program_id(0) == 0)
    def _():
        factor = BLKS * NSEQ / OBS
        lead = mail_ref[:, :16].astype(jnp.float32)
        level = (lead[:, 8:12] + lead[:, 4:8]) + lead[:, 0:4]
        top = jnp.max(level, axis=0)
        total = top + jnp.log(jnp.sum(jnp.exp(level - top[None]), axis=0))
        share = jnp.exp(level - total[None])
        tail = mail_ref[:, 16:].astype(jnp.float32)
        own = jnp.sum((tail[:, 4:8] + tail[:, 0:4]) * share, axis=1)
        other = jnp.sum((tail[:, 12:16] + tail[:, 8:12]) * share, axis=1)
        far = half_ref[0] == 0
        rows = jnp.concatenate(
            [jnp.where(far, other, own), jnp.where(far, own, other)], axis=0
        )
        lined = lax.dot_general(
            jnp.ones((8, 128), jnp.float32),
            rows,
            NT,
            precision=lax.Precision.HIGHEST,
            preferred_element_type=jnp.float32,
        )
        recv_ref[...] = (lined[0:1] * factor).astype(jnp.bfloat16)
        mine = jnp.exp(stats_ref[0:4] - total)
        row = lax.broadcasted_iota(jnp.int32, (HEADS, 4 * 128), 0)
        lane = lax.broadcasted_iota(jnp.int32, (HEADS, 4 * 128), 1)
        chosen = (lane // OBS == row).astype(jnp.float32)
        parts = []
        for b in range(BLKS):
            part = stats_ref[4 + 4 * b : 8 + 4 * b] * mine
            parts.append(jnp.concatenate([part[r : r + 1] for r in range(4)], axis=1))
        table = jnp.concatenate(parts + parts, axis=0)
        scores = lax.dot_general(
            table,
            chosen,
            NT,
            precision=lax.Precision.HIGHEST,
            preferred_element_type=jnp.float32,
        )
        block_ref[...] = scores[:BLKS] * factor


def place_last(half, got, stats, earlier):
    shape = jax.ShapeDtypeStruct((NSEQ, BLOCK, HD), jnp.bfloat16)
    out_spec = pl.BlockSpec((CHUNK, BLOCK, HD), lambda i, half: (half[0] * (HALF // CHUNK) + i, 0, 0))
    return pl.pallas_call(
        last_kernel,
        out_shape=(
            shape,
            shape,
            jax.ShapeDtypeStruct((1, NSEQ), jnp.bfloat16),
            jax.ShapeDtypeStruct((BLKS, HEADS), jnp.float32),
        ),
        grid_spec=pltpu.PrefetchScalarGridSpec(
            num_scalar_prefetch=1,
            grid=(HALF // CHUNK,),
            in_specs=[
                pl.BlockSpec((CHUNK, 2 * BLOCK, HD), lambda i, half: (i, 0, 0)),
                pl.BlockSpec((HALF, 32, HD), lambda i, half: (0, 2 * BLOCK // 32, 0)),
                pl.BlockSpec((24, 128), lambda i, half: (0, 0)),
                ANY,
                ANY,
            ],
            out_specs=(
                out_spec,
                out_spec,
                pl.BlockSpec((1, NSEQ), lambda i, half: (0, 0)),
                pl.BlockSpec((BLKS, HEADS), lambda i, half: (0, 0)),
            ),
        ),
        input_output_aliases={4: 0, 5: 1},
        cost_estimate=pl.CostEstimate(flops=0, bytes_accessed=4 * 1024 * 1024, transcendentals=0),
        name="place_last",
    )(half, got, got, stats, *earlier)


def spread(tail):
    me = lax.axis_index(SEQ)
    held = jnp.where(me == NSEQ - 1, tail, jnp.zeros_like(tail))

    def at(zh, y, x, c):
        return ((zh * 4 + y) * 4 + x) * 2 + c

    four, two = range(4), range(2)
    steps = (
        [[(at(1, 3, 3, 1), at(0, 3, 3, 1))]],
        [[(at(z, 3, 3, 1), at(z, y, 3, 1)) for z in two] for y in range(3)],
        [[(at(z, y, 3, 1), at(z, y, x, 1)) for z in two for y in four] for x in range(3)],
        [[(at(z, y, x, 1), at(z, y, x, 0)) for z in two for y in four for x in four]],
    )
    for step in steps:
        came = [lax.ppermute(held, SEQ, pairs) for pairs in step]
        for part in came:
            held = held + part
    return held


def shards(queries, keys, values, kept_index, kept_count, owner):
    position = lax.axis_index(SEQ)
    zh = lax.axis_index("zh")
    pos = position.reshape(1).astype(jnp.int32)
    near_half = zh.reshape(1).astype(jnp.int32)
    base = near_half * HALF
    slot_ids = jnp.arange(KEEP, dtype=jnp.int32)[:, None]
    owners = jnp.transpose(owner, (0, 2, 1))[0]
    picks = jnp.transpose(kept_index, (0, 2, 1))[0]
    meta = jnp.concatenate([jnp.where(slot_ids < kept_count, owners, -1), picks], axis=0)

    def exchange(packed):
        return lax.all_to_all(packed, PLANE, split_axis=0, concat_axis=0, tiled=True)

    swap = [(0, 1), (1, 0)]
    observers = spread(queries[SHARD - OBS :])
    packed, pair = pack_near(base, meta, keys, values)
    near = exchange(packed)
    other_meta = lax.ppermute(meta, "zh", swap)
    other_pair = lax.ppermute(pair, "zh", swap)

    hops = [(i, i + 1) for i in range(NSEQ - 1)]
    held = [pair]
    for _ in range(1, CYCLE):
        held.append(lax.ppermute(held[-1], SEQ, hops))

    stats = observe(pos, observers, keys)
    other_stats = lax.ppermute(stats, "zh", swap)
    far = exchange(pack_far(base, meta, other_meta, other_pair, stats, other_stats))
    attended = attend(pos, queries, held)
    first = place_near(near_half, near)
    recv_keys, recv_values, recv_scores, scores_here = place_last(1 - near_half, far, stats, first)
    return (
        attended,
        scores_here.T,
        recv_keys.reshape(1, 1, NSEQ, 1, BLOCK, HD),
        recv_values.reshape(1, 1, NSEQ, 1, BLOCK, HD),
        recv_scores.reshape(1, 1, NSEQ, 1),
    )


def solution(mesh):
    fine = Mesh(mesh.devices.reshape(2, 4, 4, 2, 4), SEQ + ("kv",))
    placed = (
        P(SEQ, "kv"),
        P(SEQ, "kv"),
        P(SEQ, "kv"),
        P(SEQ, "kv", None),
        P(SEQ, "kv"),
        P(SEQ, "kv", None),
    )
    return jax.shard_map(
        shards,
        mesh=fine,
        in_specs=placed,
        out_specs=(
            P(SEQ, "kv"),
            P("kv", SEQ),
            P(SEQ, "kv", None, None, None, None),
            P(SEQ, "kv", None, None, None, None),
            P(SEQ, "kv", None, None),
        ),
        check_vma=False,
    )
```

```python
import functools
import math

import jax
import jax.numpy as jnp
from jax import lax
from jax.experimental import pallas as pl
from jax.experimental.pallas import tpu as pltpu
from jax.sharding import Mesh, PartitionSpec as P

HD = 128
CYCLE = 4
OBS = 64
BLOCK = 128
SHARD = 512
HEADS = 8
KVS = 2
GROUP = 4
KEEP = 4
BLKS = 4
NSEQ = 64
HALF = 32
SEQ = ("zh", "y", "x", "c")
PLANE = ("y", "x", "c")
LOG2E = 1.4426950408889634
COEF = LOG2E / math.sqrt(HD)
SCALE = 1.0 / math.sqrt(HD)
BIG = 1e30
NT = (((1,), (1,)), ((), ()))


def f32dot(a, b, dims):
    return lax.dot_general(a, b, dims, preferred_element_type=jnp.float32)


def attend_kernel(pos_ref, q_ref, k0, v0, k1, v1, k2, v2, k3, v3, o_ref):
    pos = pos_ref[0]
    half = SHARD // 2
    ones = jnp.ones((SHARD, HD), jnp.bfloat16)
    vext = [jnp.concatenate([v[...], ones], axis=1) for v in (v0, v1, v2, v3)]
    row = lax.broadcasted_iota(jnp.int32, (half, half), 0)
    col = lax.broadcasted_iota(jnp.int32, (half, half), 1)
    causal = col <= row
    for tile in range(2):
        q = q_ref[tile * half : (tile + 1) * half, :]
        diag = f32dot(q, k0[tile * half : (tile + 1) * half, :], NT)
        diag = jnp.where(causal, diag, -BIG)
        peak = jnp.max(diag, axis=1, keepdims=True)
        full = []
        if tile == 1:
            own = f32dot(q, k0[:half, :], NT)
            peak = jnp.maximum(peak, jnp.max(own, axis=1, keepdims=True))
            full.append(own)
        past = [f32dot(q, k[...], NT) for k in (k1, k2, k3)]
        for distance, score in enumerate(past, 1):
            here = jnp.max(score, axis=1, keepdims=True)
            peak = jnp.where(pos >= distance, jnp.maximum(peak, here), peak)
        shift = peak * COEF
        weight = jnp.exp2(diag * COEF - shift).astype(jnp.bfloat16)
        acc = f32dot(weight, vext[0][tile * half : (tile + 1) * half], (((1,), (0,)), ((), ())))
        if tile == 1:
            weight = jnp.exp2(full[0] * COEF - shift).astype(jnp.bfloat16)
            acc += f32dot(weight, vext[0][:half], (((1,), (0,)), ((), ())))
        for distance, score in enumerate(past, 1):
            lift = jnp.where(pos >= distance, shift, BIG)
            weight = jnp.exp2(score * COEF - lift).astype(jnp.bfloat16)
            acc += f32dot(weight, vext[distance], (((1,), (0,)), ((), ())))
        mixed = acc[:, :HD] / acc[:, HD:]
        o_ref[tile * half : (tile + 1) * half, :] = mixed.astype(jnp.bfloat16)


def attend(position, queries, pairs):
    kv_spec = pl.BlockSpec((SHARD, HD), lambda h: (0, h // GROUP))
    return pl.pallas_call(
        attend_kernel,
        grid=(HEADS,),
        out_shape=jax.ShapeDtypeStruct((SHARD, HEADS * HD), jnp.bfloat16),
        in_specs=[
            pl.BlockSpec(memory_space=pltpu.SMEM),
            pl.BlockSpec((SHARD, HD), lambda h: (0, h)),
        ]
        + [kv_spec] * (2 * CYCLE),
        out_specs=pl.BlockSpec((SHARD, HD), lambda h: (0, h)),
        compiler_params=pltpu.CompilerParams(vmem_limit_bytes=32 * 1024 * 1024),
        cost_estimate=pl.CostEstimate(
            flops=HEADS * SHARD * SHARD * 4 * HD * 4,
            bytes_accessed=4 * 1024 * 1024,
            transcendentals=HEADS * SHARD * SHARD * 4,
        ),
        name="attend",
    )(position, queries, *[part for pair in pairs for part in pair])


SMEM = pl.BlockSpec(memory_space=pltpu.SMEM)
VMEM = pl.BlockSpec(memory_space=pltpu.VMEM)
ANY = pl.BlockSpec(memory_space=pl.ANY)


def seats(base, meta_ref, put):
    for head in range(HEADS):
        for c in range(KEEP):
            seat = meta_ref[c, head] - base
            unit = meta_ref[KEEP + c, head]
            pl.when((seat >= 0) & (seat < HALF))(functools.partial(put, seat, unit, head))


def block_rows(unit, start):
    return pl.ds(pl.multiple_of(unit * BLOCK + start, BLOCK), BLOCK)


def near_kernel(base_ref, meta_ref, k_ref, v_ref, out_ref, pair_ref):
    pair_ref[:SHARD] = k_ref[...]
    pair_ref[SHARD:] = v_ref[...]
    out_ref[...] = jnp.zeros_like(out_ref)

    def put(seat, unit, head):
        cols = slice((head // GROUP) * HD, (head // GROUP + 1) * HD)
        out_ref[seat, :BLOCK] = k_ref[block_rows(unit, 0), cols]
        out_ref[seat, BLOCK:] = v_ref[block_rows(unit, 0), cols]

    seats(base_ref[0], meta_ref, put)


def pack_near(base, meta, keys, values):
    return pl.pallas_call(
        near_kernel,
        out_shape=(
            jax.ShapeDtypeStruct((HALF, 2 * BLOCK, HD), jnp.bfloat16),
            jax.ShapeDtypeStruct((2 * SHARD, KVS * HD), jnp.bfloat16),
        ),
        in_specs=[SMEM, SMEM, VMEM, VMEM],
        out_specs=(VMEM, VMEM),
        compiler_params=pltpu.CompilerParams(vmem_limit_bytes=16 * 1024 * 1024),
        cost_estimate=pl.CostEstimate(flops=0, bytes_accessed=3 * 1024 * 1024, transcendentals=0),
        name="pack_near",
    )(base, meta, keys, values)


def terms(value, count):
    parts = []
    for _ in range(count):
        part = value.astype(jnp.bfloat16)
        parts.append(part)
        value = value - part.astype(jnp.float32)
    return parts


def far_kernel(
    base_ref, meta_ref, other_meta_ref, pair_ref, stats_ref, other_ref, _k, _v, out_ref, tile_ref
):
    level, other_level = stats_ref[0:4], other_ref[0:4]
    top = jnp.maximum(level, other_level)
    both = top + jnp.log(jnp.exp(level - top) + jnp.exp(other_level - top))
    part, other_part = jnp.exp(level - both), jnp.exp(other_level - both)
    blank = jnp.zeros((4, 128), jnp.float32)
    as_rows = lambda pieces: jnp.concatenate([p.astype(jnp.float32) for p in pieces], axis=0)
    for b in range(BLKS):
        rows = slice(4 + 4 * b, 8 + 4 * b)
        tile_ref[0, b] = as_rows(terms(stats_ref[rows] * part, 2) + [blank, blank])
        tile_ref[1, b] = as_rows([blank, blank] + terms(other_ref[rows] * other_part, 2))
    out_ref[:, : 2 * BLOCK, :] = jnp.zeros((HALF, 2 * BLOCK, HD), jnp.bfloat16)
    lead = as_rows(terms(both, 3) + [blank]).astype(jnp.bfloat16)
    out_ref[:, 2 * BLOCK : 2 * BLOCK + 16, :] = jnp.broadcast_to(lead[None], (HALF, 16, HD))
    out_ref[:, 2 * BLOCK + 16 :, :] = jnp.zeros((HALF, 16, HD), jnp.bfloat16)
    row = lax.broadcasted_iota(jnp.int32, (16, 128), 0)
    lane = lax.broadcasted_iota(jnp.int32, (16, 128), 1)
    which = lax.rem(row, 4) * 2 + lane // OBS
    tail = slice(2 * BLOCK + 16, 2 * BLOCK + 32)

    def add_score(source, seat, unit, head):
        picked = jnp.where(which == head, tile_ref[source, unit], 0.0).astype(jnp.bfloat16)
        out_ref[seat, tail] = out_ref[seat, tail] + picked

    def put(seat, unit, head):
        cols = slice((head // GROUP) * HD, (head // GROUP + 1) * HD)
        out_ref[seat, :BLOCK] = pair_ref[block_rows(unit, 0), cols]
        out_ref[seat, BLOCK : 2 * BLOCK] = pair_ref[block_rows(unit, SHARD), cols]
        add_score(1, seat, unit, head)

    seats(base_ref[0], meta_ref, functools.partial(add_score, 0))
    seats(base_ref[0], other_meta_ref, put)


def pack_far(base, meta, other_meta, other_pair, stats, other_stats, last):
    return pl.pallas_call(
        far_kernel,
        out_shape=jax.ShapeDtypeStruct((HALF, 2 * BLOCK + 32, HD), jnp.bfloat16),
        in_specs=[SMEM, SMEM, SMEM, VMEM, VMEM, VMEM, ANY, ANY],
        out_specs=VMEM,
        scratch_shapes=[pltpu.VMEM((2, BLKS, 16, 128), jnp.float32)],
        compiler_params=pltpu.CompilerParams(vmem_limit_bytes=16 * 1024 * 1024),
        cost_estimate=pl.CostEstimate(flops=0, bytes_accessed=3 * 1024 * 1024, transcendentals=0),
        name="pack_far",
    )(base, meta, other_meta, other_pair, stats, other_stats, *last)


def observe_kernel(pos_ref, q_ref, k_ref, stats_ref):
    pos = pos_ref[0]
    rows = [[] for _ in range(1 + BLKS)]
    for kv in range(KVS):
        heads = [
            q_ref[:, (kv * GROUP + g) * HD : (kv * GROUP + g + 1) * HD] for g in range(GROUP)
        ]
        stacked = jnp.concatenate(heads, axis=0)
        score = f32dot(k_ref[:, kv * HD : (kv + 1) * HD], stacked, NT) * SCALE
        key = lax.broadcasted_iota(jnp.int32, score.shape, 0)
        lane = lax.broadcasted_iota(jnp.int32, score.shape, 1)
        limit = (NSEQ - pos) * SHARD - OBS + lax.rem(lane, OBS)
        score = jnp.where(key <= limit, score, -jnp.inf)
        peak = jnp.max(score, axis=0, keepdims=True)
        expo = jnp.exp(score - peak)
        sums = [
            jnp.sum(expo[b * BLOCK : (b + 1) * BLOCK], axis=0, keepdims=True) for b in range(BLKS)
        ]
        mass = (sums[0] + sums[1]) + (sums[2] + sums[3])
        level = peak + jnp.log(mass)
        for side in range(2):
            cut = slice(side * 128, (side + 1) * 128)
            rows[0].append(level[:, cut])
            for b in range(BLKS):
                rows[1 + b].append((sums[b] / mass)[:, cut])
    for place_, pieces in enumerate(rows):
        stats_ref[4 * place_ : 4 * place_ + 4] = jnp.concatenate(pieces, axis=0)
    stats_ref[20:24] = jnp.zeros((4, 128), jnp.float32)


def observe(position, observers, keys):
    return pl.pallas_call(
        observe_kernel,
        out_shape=jax.ShapeDtypeStruct((24, 128), jnp.float32),
        in_specs=[SMEM, VMEM, VMEM],
        out_specs=VMEM,
        compiler_params=pltpu.CompilerParams(vmem_limit_bytes=16 * 1024 * 1024),
        name="observe",
    )(position, observers, keys)


def deliver(half, got_ref, key_ref, value_ref, sems):
    rows = pl.ds(half * HALF, HALF)
    return (
        pltpu.make_async_copy(got_ref.at[:, :BLOCK], key_ref.at[rows], sems.at[0]),
        pltpu.make_async_copy(got_ref.at[:, BLOCK : 2 * BLOCK], value_ref.at[rows], sems.at[1]),
    )


def place_kernel(half_ref, got_ref, key_ref, value_ref, sems):
    copies = deliver(half_ref[0], got_ref, key_ref, value_ref, sems)
    for copy in copies:
        copy.start()
    for copy in copies:
        copy.wait()


def place_near(half, got):
    shape = jax.ShapeDtypeStruct((NSEQ, BLOCK, HD), jnp.bfloat16)
    return pl.pallas_call(
        place_kernel,
        out_shape=(shape, shape),
        in_specs=[SMEM, VMEM],
        out_specs=(ANY, ANY),
        scratch_shapes=[pltpu.SemaphoreType.DMA((2,))],
        compiler_params=pltpu.CompilerParams(vmem_limit_bytes=16 * 1024 * 1024),
        cost_estimate=pl.CostEstimate(flops=0, bytes_accessed=4 * 1024 * 1024, transcendentals=0),
        name="place_near",
    )(half, got)


def last_kernel(
    half_ref, got_ref, stats_ref, _k, _v, key_ref, value_ref, recv_ref, block_ref, sems
):
    copies = deliver(half_ref[0], got_ref, key_ref, value_ref, sems)
    for copy in copies:
        copy.start()
    factor = BLKS * NSEQ / OBS
    lead = got_ref[:, 2 * BLOCK : 2 * BLOCK + 16].astype(jnp.float32)
    level = (lead[:, 8:12] + lead[:, 4:8]) + lead[:, 0:4]
    top = jnp.max(level, axis=0)
    total = top + jnp.log(jnp.sum(jnp.exp(level - top[None]), axis=0))
    share = jnp.exp(level - total[None])
    tail = got_ref[:, 2 * BLOCK + 16 :].astype(jnp.float32)
    own = jnp.sum((tail[:, 4:8] + tail[:, 0:4]) * share, axis=1)
    other = jnp.sum((tail[:, 12:16] + tail[:, 8:12]) * share, axis=1)
    far = half_ref[0] == 0
    rows = jnp.concatenate(
        [jnp.where(far, other, own), jnp.where(far, own, other)], axis=0
    )
    lined = lax.dot_general(
        jnp.ones((8, 128), jnp.float32),
        rows,
        NT,
        precision=lax.Precision.HIGHEST,
        preferred_element_type=jnp.float32,
    )
    recv_ref[...] = (lined[0:1] * factor).astype(jnp.bfloat16)
    mine = jnp.exp(stats_ref[0:4] - total)
    row = lax.broadcasted_iota(jnp.int32, (HEADS, 4 * 128), 0)
    lane = lax.broadcasted_iota(jnp.int32, (HEADS, 4 * 128), 1)
    chosen = (lane // OBS == row).astype(jnp.float32)
    parts = []
    for b in range(BLKS):
        part = stats_ref[4 + 4 * b : 8 + 4 * b] * mine
        parts.append(jnp.concatenate([part[r : r + 1] for r in range(4)], axis=1))
    table = jnp.concatenate(parts + parts, axis=0)
    scores = lax.dot_general(
        table,
        chosen,
        NT,
        precision=lax.Precision.HIGHEST,
        preferred_element_type=jnp.float32,
    )
    block_ref[...] = scores[:BLKS] * factor
    for copy in copies:
        copy.wait()


def place_last(half, got, stats, earlier):
    shape = jax.ShapeDtypeStruct((NSEQ, BLOCK, HD), jnp.bfloat16)
    return pl.pallas_call(
        last_kernel,
        out_shape=(
            shape,
            shape,
            jax.ShapeDtypeStruct((1, NSEQ), jnp.bfloat16),
            jax.ShapeDtypeStruct((BLKS, HEADS), jnp.float32),
        ),
        in_specs=[SMEM, VMEM, VMEM, ANY, ANY],
        out_specs=(ANY, ANY, VMEM, VMEM),
        scratch_shapes=[pltpu.SemaphoreType.DMA((2,))],
        input_output_aliases={3: 0, 4: 1},
        compiler_params=pltpu.CompilerParams(vmem_limit_bytes=16 * 1024 * 1024),
        cost_estimate=pl.CostEstimate(flops=0, bytes_accessed=4 * 1024 * 1024, transcendentals=0),
        name="place_last",
    )(half, got, stats, *earlier)


def spread(tail):
    me = lax.axis_index(SEQ)
    held = jnp.where(me == NSEQ - 1, tail, jnp.zeros_like(tail))

    def at(zh, y, x, c):
        return ((zh * 4 + y) * 4 + x) * 2 + c

    four, two = range(4), range(2)
    steps = (
        [[(at(1, 3, 3, 1), at(0, 3, 3, 1))]],
        [[(at(z, 3, 3, 1), at(z, y, 3, 1)) for z in two] for y in range(3)],
        [[(at(z, y, 3, 1), at(z, y, x, 1)) for z in two for y in four] for x in range(3)],
        [[(at(z, y, x, 1), at(z, y, x, 0)) for z in two for y in four for x in four]],
    )
    for step in steps:
        came = [lax.ppermute(held, SEQ, pairs) for pairs in step]
        for part in came:
            held = held + part
    return held


def shards(queries, keys, values, kept_index, kept_count, owner):
    position = lax.axis_index(SEQ)
    zh = lax.axis_index("zh")
    pos = position.reshape(1).astype(jnp.int32)
    near_half = zh.reshape(1).astype(jnp.int32)
    base = near_half * HALF
    slot_ids = jnp.arange(KEEP, dtype=jnp.int32)[:, None]
    owners = jnp.transpose(owner, (0, 2, 1))[0]
    picks = jnp.transpose(kept_index, (0, 2, 1))[0]
    meta = jnp.concatenate([jnp.where(slot_ids < kept_count, owners, -1), picks], axis=0)

    def exchange(packed):
        return lax.all_to_all(packed, PLANE, split_axis=0, concat_axis=0, tiled=True)

    swap = [(0, 1), (1, 0)]
    observers = spread(queries[SHARD - OBS :])
    packed, pair = pack_near(base, meta, keys, values)
    near = exchange(packed)
    other_meta = lax.ppermute(meta, "zh", swap)
    other_pair = lax.ppermute(pair, "zh", swap)

    hops = [(i, i + 1) for i in range(NSEQ - 1)]
    held = [(keys, values)]
    for _ in range(1, CYCLE):
        held.append(tuple(lax.ppermute(part, SEQ, hops) for part in held[-1]))

    stats = observe(pos, observers, keys)
    other_stats = lax.ppermute(stats, "zh", swap)
    far = exchange(
        pack_far(base, meta, other_meta, other_pair, stats, other_stats, held[-1])
    )
    attended = attend(pos, queries, held)
    first = place_near(near_half, near)
    recv_keys, recv_values, recv_scores, scores_here = place_last(1 - near_half, far, stats, first)
    return (
        attended,
        scores_here.T,
        recv_keys.reshape(1, 1, NSEQ, 1, BLOCK, HD),
        recv_values.reshape(1, 1, NSEQ, 1, BLOCK, HD),
        recv_scores.reshape(1, 1, NSEQ, 1),
    )


def solution(mesh):
    fine = Mesh(mesh.devices.reshape(2, 4, 4, 2, 4), SEQ + ("kv",))
    placed = (
        P(SEQ, "kv"),
        P(SEQ, "kv"),
        P(SEQ, "kv"),
        P(SEQ, "kv", None),
        P(SEQ, "kv"),
        P(SEQ, "kv", None),
    )
    return jax.shard_map(
        shards,
        mesh=fine,
        in_specs=placed,
        out_specs=(
            P(SEQ, "kv"),
            P("kv", SEQ),
            P(SEQ, "kv", None, None, None, None),
            P(SEQ, "kv", None, None, None, None),
            P(SEQ, "kv", None, None),
        ),
        check_vma=False,
    )
```

```python
import functools
import math

import jax
import jax.numpy as jnp
from jax import lax
from jax.experimental import pallas as pl
from jax.experimental.pallas import tpu as pltpu
from jax.sharding import Mesh, PartitionSpec as P

HD = 128
CYCLE = 4
OBS = 64
BLOCK = 128
SHARD = 512
HEADS = 8
KVS = 2
GROUP = 4
KEEP = 4
BLKS = 4
NSEQ = 64
HALF = 32
SEQ = ("zh", "y", "x", "c")
PLANE = ("y", "x", "c")
LEAD = 4 * BLOCK
SHIFT = 2
LOG2E = 1.4426950408889634
COEF = LOG2E / math.sqrt(HD)
SCALE = 1.0 / math.sqrt(HD)
BIG = 1e30
NT = (((1,), (1,)), ((), ()))
NN = (((1,), (0,)), ((), ()))


def f32dot(a, b, dims):
    return lax.dot_general(a, b, dims, preferred_element_type=jnp.float32)


def attend_kernel(pos_ref, q_ref, *refs):
    o_ref = refs[-1]
    pos = pos_ref[0]
    p0, p1, p2, p3, held, ea, eb = [refs[2 * i : 2 * i + 2] for i in range(7)]
    first = pos - NSEQ // 2
    keys, values = [p0[0][...]], [p0[1][...]]
    for side, out in ((0, keys), (1, values)):
        near = [p[side][...] for p in (p1, p2, p3)]
        other, swapped, edge = [e[side][...] for e in (held, ea, eb)]
        out.append(jnp.where(first == 0, swapped, near[0]))
        out.append(jnp.where((first == 0) | (first == 1), other, near[1]))
        third = jnp.where((first == 0) | (first == 2), edge, near[2])
        out.append(jnp.where(first == 1, swapped, third))
    half = SHARD // 2
    ones = jnp.ones((SHARD, HD), jnp.bfloat16)
    vext = [jnp.concatenate([v, ones], axis=1) for v in values]
    row = lax.broadcasted_iota(jnp.int32, (half, half), 0)
    col = lax.broadcasted_iota(jnp.int32, (half, half), 1)
    causal = col <= row
    for tile in range(2):
        q = q_ref[tile * half : (tile + 1) * half, :]
        diag = f32dot(q, keys[0][tile * half : (tile + 1) * half, :], NT)
        diag = jnp.where(causal, diag, -BIG)
        peak = jnp.max(diag, axis=1, keepdims=True)
        if tile == 1:
            own = f32dot(q, keys[0][:half, :], NT)
            peak = jnp.maximum(peak, jnp.max(own, axis=1, keepdims=True))
        past = [f32dot(q, k, NT) for k in keys[1:]]
        for distance, score in enumerate(past, 1):
            here = jnp.max(score, axis=1, keepdims=True)
            peak = jnp.where(pos >= distance, jnp.maximum(peak, here), peak)
        shift = peak * COEF
        weight = jnp.exp2(diag * COEF - shift).astype(jnp.bfloat16)
        acc = f32dot(weight, vext[0][tile * half : (tile + 1) * half], NN)
        if tile == 1:
            weight = jnp.exp2(own * COEF - shift).astype(jnp.bfloat16)
            acc += f32dot(weight, vext[0][:half], NN)
        for distance, score in enumerate(past, 1):
            lift = jnp.where(pos >= distance, shift, BIG)
            weight = jnp.exp2(score * COEF - lift).astype(jnp.bfloat16)
            acc += f32dot(weight, vext[distance], NN)
        mixed = acc[:, :HD] / acc[:, HD:]
        o_ref[tile * half : (tile + 1) * half, :] = mixed.astype(jnp.bfloat16)


def attend(position, queries, pairs):
    key_spec = pl.BlockSpec((SHARD, HD), lambda h: (0, h // GROUP))
    value_spec = pl.BlockSpec((SHARD, HD), lambda h: (1, h // GROUP))
    return pl.pallas_call(
        attend_kernel,
        grid=(HEADS,),
        out_shape=jax.ShapeDtypeStruct((SHARD, HEADS * HD), jnp.bfloat16),
        in_specs=[
            pl.BlockSpec(memory_space=pltpu.SMEM),
            pl.BlockSpec((SHARD, HD), lambda h: (0, h)),
        ]
        + [key_spec, value_spec] * len(pairs),
        out_specs=pl.BlockSpec((SHARD, HD), lambda h: (0, h)),
        compiler_params=pltpu.CompilerParams(vmem_limit_bytes=32 * 1024 * 1024),
        cost_estimate=pl.CostEstimate(
            flops=HEADS * SHARD * SHARD * 4 * HD * 4,
            bytes_accessed=4 * 1024 * 1024,
            transcendentals=HEADS * SHARD * SHARD * 4,
        ),
        name="attend",
    )(position, queries, *[pair for pair in pairs for _ in range(2)])


SMEM = pl.BlockSpec(memory_space=pltpu.SMEM)
VMEM = pl.BlockSpec(memory_space=pltpu.VMEM)
ANY = pl.BlockSpec(memory_space=pl.ANY)


def join_kernel(k_ref, v_ref, pair_ref, sems):
    copies = (
        pltpu.make_async_copy(k_ref, pair_ref.at[:SHARD], sems.at[0]),
        pltpu.make_async_copy(v_ref, pair_ref.at[SHARD:], sems.at[1]),
    )
    for copy in copies:
        copy.start()
    for copy in copies:
        copy.wait()


def join(keys, values):
    return pl.pallas_call(
        join_kernel,
        out_shape=jax.ShapeDtypeStruct((2 * SHARD, KVS * HD), jnp.bfloat16),
        in_specs=[ANY, ANY],
        out_specs=VMEM,
        scratch_shapes=[pltpu.SemaphoreType.DMA((2,))],
        cost_estimate=pl.CostEstimate(flops=0, bytes_accessed=1024 * 1024, transcendentals=0),
        name="join",
    )(keys, values)


def seats(entry, put):
    for head in range(HEADS):
        for c in range(KEEP):
            seat, unit = entry(c, head)
            pl.when((seat >= 0) & (seat < HALF))(functools.partial(put, seat, unit, head))


def block_rows(unit, start):
    return pl.ds(pl.multiple_of(unit * BLOCK + start, BLOCK), BLOCK)


def terms(value, count):
    parts = []
    for _ in range(count):
        part = value.astype(jnp.bfloat16)
        parts.append(part)
        value = value - part.astype(jnp.float32)
    return parts


def pack_kernel(base_ref, meta_ref, list_ref, pair_ref, other_ref, mail_ref, got_ref, *refs):
    out_ref, stats_ref, tile_ref = refs[-3:]
    last = base_ref[0] > 0
    mine = jnp.where(last, mail_ref[0:24], got_ref[24:48])
    other = jnp.where(last, mail_ref[24:48], got_ref[0:24])
    stats_ref[...] = mine
    level, other_level = mine[0:4], other[0:4]
    top = jnp.maximum(level, other_level)
    both = top + jnp.log(jnp.exp(level - top) + jnp.exp(other_level - top))
    part, other_part = jnp.exp(level - both), jnp.exp(other_level - both)
    blank = jnp.zeros((4, 128), jnp.float32)
    as_rows = lambda pieces: jnp.concatenate([p.astype(jnp.float32) for p in pieces], axis=0)
    for b in range(BLKS):
        rows = slice(4 + 4 * b, 8 + 4 * b)
        tile_ref[0, b] = as_rows(terms(mine[rows] * part, 2) + [blank, blank])
        tile_ref[1, b] = as_rows([blank, blank] + terms(other[rows] * other_part, 2))
    out_ref[:, :LEAD, :] = jnp.zeros((HALF, LEAD, HD), jnp.bfloat16)
    lead = as_rows(terms(both, 3) + [blank]).astype(jnp.bfloat16)
    out_ref[:, LEAD : LEAD + 16, :] = jnp.broadcast_to(lead[None], (HALF, 16, HD))
    out_ref[:, LEAD + 16 :, :] = jnp.zeros((HALF, 16, HD), jnp.bfloat16)
    row = lax.broadcasted_iota(jnp.int32, (16, 128), 0)
    lane = lax.broadcasted_iota(jnp.int32, (16, 128), 1)
    which = lax.rem(row, 4) * 2 + lane // OBS
    tail = slice(LEAD + 16, LEAD + 32)

    def my_entry(c, head):
        return meta_ref[c, head] - base_ref[0], meta_ref[KEEP + c, head]

    def other_entry(c, head):
        seat = list_ref[c, head].astype(jnp.int32) - base_ref[0]
        return seat, list_ref[KEEP + c, head].astype(jnp.int32)

    def add_score(source, seat, unit, head):
        picked = jnp.where(which == head, tile_ref[source, unit], 0.0).astype(jnp.bfloat16)
        out_ref[seat, tail] = out_ref[seat, tail] + picked

    def put(source, held_ref, seat, unit, head):
        cols = slice((head // GROUP) * HD, (head // GROUP + 1) * HD)
        start = 2 * BLOCK * source
        out_ref[seat, start : start + BLOCK] = held_ref[block_rows(unit, 0), cols]
        out_ref[seat, start + BLOCK : start + 2 * BLOCK] = held_ref[block_rows(unit, SHARD), cols]
        add_score(source, seat, unit, head)

    seats(my_entry, functools.partial(put, 0, pair_ref))
    seats(other_entry, functools.partial(put, 1, other_ref))


def pack(base, meta, pair, other_pair, mail, got, after):
    return pl.pallas_call(
        pack_kernel,
        out_shape=(
            jax.ShapeDtypeStruct((HALF, LEAD + 32, HD), jnp.bfloat16),
            jax.ShapeDtypeStruct((24, 128), jnp.float32),
        ),
        in_specs=[SMEM, SMEM, SMEM, VMEM, VMEM, VMEM, VMEM] + [ANY] * len(after),
        out_specs=(VMEM, VMEM),
        scratch_shapes=[pltpu.VMEM((2, BLKS, 16, 128), jnp.float32)],
        compiler_params=pltpu.CompilerParams(vmem_limit_bytes=16 * 1024 * 1024),
        cost_estimate=pl.CostEstimate(flops=0, bytes_accessed=3 * 1024 * 1024, transcendentals=0),
        name="pack",
    )(base, meta, got[48:56], pair, other_pair, mail, got, *after)


def score_keys(pos, q_ref, k_ref, mail_ref, start):
    rows = [[] for _ in range(1 + BLKS)]
    for kv in range(KVS):
        heads = [
            q_ref[:, (kv * GROUP + g) * HD : (kv * GROUP + g + 1) * HD] for g in range(GROUP)
        ]
        stacked = jnp.concatenate(heads, axis=0)
        score = f32dot(k_ref[:SHARD, kv * HD : (kv + 1) * HD], stacked, NT) * SCALE
        key = lax.broadcasted_iota(jnp.int32, score.shape, 0)
        lane = lax.broadcasted_iota(jnp.int32, score.shape, 1)
        limit = (NSEQ - pos) * SHARD - OBS + lax.rem(lane, OBS)
        score = jnp.where(key <= limit, score, -jnp.inf)
        peak = jnp.max(score, axis=0, keepdims=True)
        expo = jnp.exp(score - peak)
        sums = [
            jnp.sum(expo[b * BLOCK : (b + 1) * BLOCK], axis=0, keepdims=True) for b in range(BLKS)
        ]
        mass = (sums[0] + sums[1]) + (sums[2] + sums[3])
        level = peak + jnp.log(mass)
        for side in range(2):
            cut = slice(side * 128, (side + 1) * 128)
            rows[0].append(level[:, cut])
            for b in range(BLKS):
                rows[1 + b].append((sums[b] / mass)[:, cut])
    for place_, pieces in enumerate(rows):
        at = start + 4 * place_
        mail_ref[at : at + 4] = jnp.concatenate(pieces, axis=0)
    mail_ref[start + 20 : start + 24] = jnp.zeros((4, 128), jnp.float32)


def observe_kernel(pos_ref, q_ref, k_ref, other_ref, meta_ref, *refs):
    mail_ref = refs[-1]
    pos = pos_ref[0]
    score_keys(pos, q_ref, k_ref, mail_ref, 0)
    score_keys(0, q_ref, other_ref, mail_ref, 24)
    mail_ref[48:56] = meta_ref[...].astype(jnp.float32)


def observe(position, observers, keys, other_keys, meta, after):
    return pl.pallas_call(
        observe_kernel,
        out_shape=jax.ShapeDtypeStruct((56, 128), jnp.float32),
        in_specs=[SMEM, VMEM, VMEM, VMEM, VMEM] + [ANY] * len(after),
        out_specs=VMEM,
        compiler_params=pltpu.CompilerParams(vmem_limit_bytes=16 * 1024 * 1024),
        name="observe",
    )(position, observers, keys, other_keys, meta, *after)


def sends(half, buf_ref, key_ref, value_ref, sems):
    own, other = half * HALF, (1 - half) * HALF
    most = HALF - SHIFT
    pieces = (
        (0, 0, own, HALF),
        (1, SHIFT * half, other + SHIFT * (1 - half), most),
        (1, most * (1 - half), other + most * half, SHIFT),
    )
    copies = []
    for number, (source, start, row, count) in enumerate(pieces):
        for side, out_ref in enumerate((key_ref, value_ref)):
            at_ = (2 * source + side) * BLOCK
            copies.append(
                pltpu.make_async_copy(
                    buf_ref.at[pl.ds(start, count), at_ : at_ + BLOCK],
                    out_ref.at[pl.ds(row, count)],
                    sems.at[2 * number + side],
                )
            )
    return copies


def last_kernel(
    half_ref, got_ref, stats_ref, key_ref, value_ref, recv_ref, block_ref, sems
):
    copies = sends(half_ref[0], got_ref, key_ref, value_ref, sems)
    for copy in copies:
        copy.start()
    factor = BLKS * NSEQ / OBS
    lead = got_ref[:, LEAD : LEAD + 16].astype(jnp.float32)
    level = (lead[:, 8:12] + lead[:, 4:8]) + lead[:, 0:4]
    top = jnp.max(level, axis=0)
    total = top + jnp.log(jnp.sum(jnp.exp(level - top[None]), axis=0))
    share = jnp.exp(level - total[None])
    tail = got_ref[:, LEAD + 16 :].astype(jnp.float32)
    own = jnp.sum((tail[:, 4:8] + tail[:, 0:4]) * share, axis=1)
    other = jnp.sum((tail[:, 12:16] + tail[:, 8:12]) * share, axis=1)
    low = half_ref[0] == 0
    other = jnp.where(
        low,
        jnp.concatenate([other[HALF - SHIFT :], other[: HALF - SHIFT]], axis=0),
        jnp.concatenate([other[SHIFT:], other[:SHIFT]], axis=0),
    )
    rows = jnp.concatenate(
        [jnp.where(low, own, other), jnp.where(low, other, own)], axis=0
    )
    lined = lax.dot_general(
        jnp.ones((8, 128), jnp.float32),
        rows,
        NT,
        precision=lax.Precision.HIGHEST,
        preferred_element_type=jnp.float32,
    )
    recv_ref[...] = (lined[0:1] * factor).astype(jnp.bfloat16)
    mine = jnp.exp(stats_ref[0:4] - total)
    row = lax.broadcasted_iota(jnp.int32, (HEADS, 4 * 128), 0)
    lane = lax.broadcasted_iota(jnp.int32, (HEADS, 4 * 128), 1)
    chosen = (lane // OBS == row).astype(jnp.float32)
    parts = []
    for b in range(BLKS):
        part = stats_ref[4 + 4 * b : 8 + 4 * b] * mine
        parts.append(jnp.concatenate([part[r : r + 1] for r in range(4)], axis=1))
    table = jnp.concatenate(parts + parts, axis=0)
    scores = lax.dot_general(
        table,
        chosen,
        NT,
        precision=lax.Precision.HIGHEST,
        preferred_element_type=jnp.float32,
    )
    block_ref[...] = scores[:BLKS] * factor
    for copy in copies:
        copy.wait()


def place(half, got, stats):
    shape = jax.ShapeDtypeStruct((NSEQ, BLOCK, HD), jnp.bfloat16)
    return pl.pallas_call(
        last_kernel,
        out_shape=(
            shape,
            shape,
            jax.ShapeDtypeStruct((1, NSEQ), jnp.bfloat16),
            jax.ShapeDtypeStruct((BLKS, HEADS), jnp.float32),
        ),
        in_specs=[SMEM, VMEM, VMEM],
        out_specs=(ANY, ANY, VMEM, VMEM),
        scratch_shapes=[pltpu.SemaphoreType.DMA((6,))],
        compiler_params=pltpu.CompilerParams(vmem_limit_bytes=16 * 1024 * 1024),
        cost_estimate=pl.CostEstimate(flops=0, bytes_accessed=4 * 1024 * 1024, transcendentals=0),
        name="place",
    )(half, got, stats)


def at(zh, y, x, c):
    return ((zh * 4 + y) * 4 + x) * 2 + c


def spread(tail):
    me = lax.axis_index(SEQ)
    held = jnp.where(me == NSEQ - 1, tail, jnp.zeros_like(tail))
    four = range(4)
    steps = (
        [[(at(1, 3, 3, 1), at(1, y, 3, 1))] for y in range(3)],
        [[(at(1, y, 3, 1), at(1, y, x, 1)) for y in four] for x in range(3)],
        [[(at(1, y, x, 1), at(1, y, x, 0)) for y in four for x in four]],
    )
    levels = []
    for step in steps:
        came = [lax.ppermute(held, SEQ, pairs) for pairs in step]
        for part in came:
            held = held + part
        levels.append(held)
    return levels


def shards(queries, keys, values, kept_index, kept_count, owner):
    position = lax.axis_index(SEQ)
    zh = lax.axis_index("zh")
    pos = position.reshape(1).astype(jnp.int32)
    near_half = zh.reshape(1).astype(jnp.int32)
    base = near_half * HALF
    slot_ids = jnp.arange(KEEP, dtype=jnp.int32)[:, None]
    owners = jnp.transpose(owner, (0, 2, 1))[0]
    picks = jnp.transpose(kept_index, (0, 2, 1))[0]
    meta = jnp.concatenate([jnp.where(slot_ids < kept_count, owners, -1), picks], axis=0)
    meta = jnp.pad(meta, ((0, 0), (0, 128 - HEADS)))

    def exchange(packed):
        return lax.all_to_all(packed, PLANE, split_axis=0, concat_axis=0, tiled=True)

    def hop(pair, by):
        steps = [(i, i + by) for i in range(NSEQ) if i // HALF == (i + by) // HALF]
        return lax.ppermute(pair, SEQ, steps)

    swap = []
    for i in range(HALF):
        j = HALF + (i + SHIFT) % HALF
        swap += [(i, j), (j, i)]
    levels = spread(queries[SHARD - OBS :])
    pair = join(keys, values)
    other_pair = lax.ppermute(pair, SEQ, swap)
    one, two = hop(pair, 1), hop(pair, 2)
    three = hop(two, 1)
    edge_a = lax.ppermute(other_pair, SEQ, [(32, 33), (33, 32)])
    edge_b = lax.ppermute(other_pair, SEQ, [(33, 34), (63, 32)])

    mail = observe(pos, levels[-1], pair, other_pair, meta, (one, two))
    got = lax.ppermute(mail, SEQ, swap)
    packed, stats = pack(base, meta, pair, other_pair, mail, got, (three, edge_a, edge_b))
    arrived = exchange(packed)
    attended = attend(pos, queries, [pair, one, two, three, other_pair, edge_a, edge_b])
    recv_keys, recv_values, recv_scores, scores_here = place(near_half, arrived, stats)
    return (
        attended,
        scores_here.T,
        recv_keys.reshape(1, 1, NSEQ, 1, BLOCK, HD),
        recv_values.reshape(1, 1, NSEQ, 1, BLOCK, HD),
        recv_scores.reshape(1, 1, NSEQ, 1),
    )


def solution(mesh):
    fine = Mesh(mesh.devices.reshape(2, 4, 4, 2, 4), SEQ + ("kv",))
    placed = (
        P(SEQ, "kv"),
        P(SEQ, "kv"),
        P(SEQ, "kv"),
        P(SEQ, "kv", None),
        P(SEQ, "kv"),
        P(SEQ, "kv", None),
    )
    return jax.shard_map(
        shards,
        mesh=fine,
        in_specs=placed,
        out_specs=(
            P(SEQ, "kv"),
            P("kv", SEQ),
            P(SEQ, "kv", None, None, None, None),
            P(SEQ, "kv", None, None, None, None),
            P(SEQ, "kv", None, None),
        ),
        check_vma=False,
    )
```

```python
import functools
import math

import jax
import jax.numpy as jnp
from jax import lax
from jax.experimental import pallas as pl
from jax.experimental.pallas import tpu as pltpu
from jax.sharding import Mesh, PartitionSpec as P

HD = 128
CYCLE = 4
OBS = 64
BLOCK = 128
SHARD = 512
HEADS = 8
KVS = 2
GROUP = 4
KEEP = 4
BLKS = 4
NSEQ = 64
HALF = 32
SEQ = ("zh", "y", "x", "c")
PLANE = ("y", "x", "c")
PAIRS = 7
LEAD = 2 * BLOCK
SHIFT = 2
LOG2E = 1.4426950408889634
COEF = LOG2E / math.sqrt(HD)
SCALE = 1.0 / math.sqrt(HD)
BIG = 1e30
NT = (((1,), (1,)), ((), ()))
NN = (((1,), (0,)), ((), ()))


def f32dot(a, b, dims):
    return lax.dot_general(a, b, dims, preferred_element_type=jnp.float32)


def attend_kernel(pos_ref, q_from, *refs):
    o_ref, q_all, held_all, sems = refs[-4:]
    pos = pos_ref[0]
    head = pl.program_id(0)

    @pl.when(head == 0)
    def _():
        copies = [pltpu.make_async_copy(q_from, q_all, sems.at[PAIRS])]
        for i in range(PAIRS):
            copies.append(pltpu.make_async_copy(refs[i], held_all.at[i], sems.at[i]))
        for copy in copies:
            copy.start()
        for copy in copies:
            copy.wait()

    cols = pl.ds(pl.multiple_of((head // GROUP) * HD, HD), HD)
    sides = (slice(0, SHARD), slice(SHARD, 2 * SHARD))
    p0, p1, p2, p3, held, ea, eb = [
        [held_all.at[i, side, cols] for side in sides] for i in range(PAIRS)
    ]
    q_ref = q_all.at[:, pl.ds(pl.multiple_of(head * HD, HD), HD)]
    first = pos - NSEQ // 2
    keys, values = [p0[0][...]], [p0[1][...]]
    for side, out in ((0, keys), (1, values)):
        near = [p[side][...] for p in (p1, p2, p3)]
        other, swapped, edge = [e[side][...] for e in (held, ea, eb)]
        out.append(jnp.where(first == 0, swapped, near[0]))
        out.append(jnp.where((first == 0) | (first == 1), other, near[1]))
        third = jnp.where((first == 0) | (first == 2), edge, near[2])
        out.append(jnp.where(first == 1, swapped, third))
    half = SHARD // 2
    ones = jnp.ones((SHARD, HD), jnp.bfloat16)
    vext = [jnp.concatenate([v, ones], axis=1) for v in values]
    row = lax.broadcasted_iota(jnp.int32, (half, half), 0)
    col = lax.broadcasted_iota(jnp.int32, (half, half), 1)
    causal = col <= row
    for tile in range(2):
        q = q_ref[tile * half : (tile + 1) * half, :]
        diag = f32dot(q, keys[0][tile * half : (tile + 1) * half, :], NT)
        diag = jnp.where(causal, diag, -BIG)
        peak = jnp.max(diag, axis=1, keepdims=True)
        if tile == 1:
            own = f32dot(q, keys[0][:half, :], NT)
            peak = jnp.maximum(peak, jnp.max(own, axis=1, keepdims=True))
        past = [f32dot(q, k, NT) for k in keys[1:]]
        for distance, score in enumerate(past, 1):
            here = jnp.max(score, axis=1, keepdims=True)
            peak = jnp.where(pos >= distance, jnp.maximum(peak, here), peak)
        shift = peak * COEF
        weight = jnp.exp2(diag * COEF - shift).astype(jnp.bfloat16)
        acc = f32dot(weight, vext[0][tile * half : (tile + 1) * half], NN)
        if tile == 1:
            weight = jnp.exp2(own * COEF - shift).astype(jnp.bfloat16)
            acc += f32dot(weight, vext[0][:half], NN)
        for distance, score in enumerate(past, 1):
            lift = jnp.where(pos >= distance, shift, BIG)
            weight = jnp.exp2(score * COEF - lift).astype(jnp.bfloat16)
            acc += f32dot(weight, vext[distance], NN)
        mixed = acc[:, :HD] / acc[:, HD:]
        o_ref[tile * half : (tile + 1) * half, :] = mixed.astype(jnp.bfloat16)


def attend(position, queries, pairs):
    return pl.pallas_call(
        attend_kernel,
        grid=(HEADS,),
        out_shape=jax.ShapeDtypeStruct((SHARD, HEADS * HD), jnp.bfloat16),
        in_specs=[pl.BlockSpec(memory_space=pltpu.SMEM)]
        + [pl.BlockSpec(memory_space=pl.ANY)] * (1 + PAIRS),
        out_specs=pl.BlockSpec((SHARD, HD), lambda h: (0, h)),
        scratch_shapes=[
            pltpu.VMEM((SHARD, HEADS * HD), jnp.bfloat16),
            pltpu.VMEM((PAIRS, 2 * SHARD, KVS * HD), jnp.bfloat16),
            pltpu.SemaphoreType.DMA((PAIRS + 1,)),
        ],
        compiler_params=pltpu.CompilerParams(vmem_limit_bytes=60 * 1024 * 1024),
        cost_estimate=pl.CostEstimate(
            flops=HEADS * SHARD * SHARD * 4 * HD * 4,
            bytes_accessed=4 * 1024 * 1024,
            transcendentals=HEADS * SHARD * SHARD * 4,
        ),
        name="attend",
    )(position, queries, *pairs)


SMEM = pl.BlockSpec(memory_space=pltpu.SMEM)
VMEM = pl.BlockSpec(memory_space=pltpu.VMEM)
ANY = pl.BlockSpec(memory_space=pl.ANY)


def join_kernel(k_ref, v_ref, pair_ref, sems):
    copies = (
        pltpu.make_async_copy(k_ref, pair_ref.at[:SHARD], sems.at[0]),
        pltpu.make_async_copy(v_ref, pair_ref.at[SHARD:], sems.at[1]),
    )
    for copy in copies:
        copy.start()
    for copy in copies:
        copy.wait()


def join(keys, values):
    return pl.pallas_call(
        join_kernel,
        out_shape=jax.ShapeDtypeStruct((2 * SHARD, KVS * HD), jnp.bfloat16),
        in_specs=[ANY, ANY],
        out_specs=VMEM,
        scratch_shapes=[pltpu.SemaphoreType.DMA((2,))],
        cost_estimate=pl.CostEstimate(flops=0, bytes_accessed=1024 * 1024, transcendentals=0),
        name="join",
    )(keys, values)


def seats(entry, put):
    for head in range(HEADS):
        for c in range(KEEP):
            seat, unit = entry(c, head)
            pl.when((seat >= 0) & (seat < HALF))(functools.partial(put, seat, unit, head))


def block_rows(unit, start):
    return pl.ds(pl.multiple_of(unit * BLOCK + start, BLOCK), BLOCK)


def near_kernel(base_ref, meta_ref, pair_ref, *refs):
    out_ref = refs[-1]
    out_ref[...] = jnp.zeros_like(out_ref)

    def entry(c, head):
        return meta_ref[c, head] - base_ref[0], meta_ref[KEEP + c, head]

    def put(seat, unit, head):
        cols = slice((head // GROUP) * HD, (head // GROUP + 1) * HD)
        out_ref[seat, :BLOCK] = pair_ref[block_rows(unit, 0), cols]
        out_ref[seat, BLOCK:] = pair_ref[block_rows(unit, SHARD), cols]

    seats(entry, put)


def pack_near(base, meta, pair, after):
    return pl.pallas_call(
        near_kernel,
        out_shape=jax.ShapeDtypeStruct((HALF, 2 * BLOCK, HD), jnp.bfloat16),
        in_specs=[SMEM, SMEM, VMEM] + [ANY] * len(after),
        out_specs=VMEM,
        compiler_params=pltpu.CompilerParams(vmem_limit_bytes=60 * 1024 * 1024),
        cost_estimate=pl.CostEstimate(flops=0, bytes_accessed=3 * 1024 * 1024, transcendentals=0),
        name="pack_near",
    )(base, meta, pair, *after)


def terms(value, count):
    parts = []
    for _ in range(count):
        part = value.astype(jnp.bfloat16)
        parts.append(part)
        value = value - part.astype(jnp.float32)
    return parts


def far_kernel(base_ref, meta_ref, list_ref, held_ref, mail_ref, got_ref, *refs):
    out_ref, stats_ref, tile_ref = refs[-3:]
    last = base_ref[0] > 0
    mine = jnp.where(last, mail_ref[0:24], got_ref[24:48])
    other = jnp.where(last, mail_ref[24:48], got_ref[0:24])
    stats_ref[...] = mine
    level, other_level = mine[0:4], other[0:4]
    top = jnp.maximum(level, other_level)
    both = top + jnp.log(jnp.exp(level - top) + jnp.exp(other_level - top))
    part, other_part = jnp.exp(level - both), jnp.exp(other_level - both)
    blank = jnp.zeros((4, 128), jnp.float32)
    as_rows = lambda pieces: jnp.concatenate([p.astype(jnp.float32) for p in pieces], axis=0)
    for b in range(BLKS):
        rows = slice(4 + 4 * b, 8 + 4 * b)
        tile_ref[0, b] = as_rows(terms(mine[rows] * part, 2) + [blank, blank])
        tile_ref[1, b] = as_rows([blank, blank] + terms(other[rows] * other_part, 2))
    out_ref[:, :LEAD, :] = jnp.zeros((HALF, LEAD, HD), jnp.bfloat16)
    lead = as_rows(terms(both, 3) + [blank]).astype(jnp.bfloat16)
    out_ref[:, LEAD : LEAD + 16, :] = jnp.broadcast_to(lead[None], (HALF, 16, HD))
    out_ref[:, LEAD + 16 :, :] = jnp.zeros((HALF, 16, HD), jnp.bfloat16)
    row = lax.broadcasted_iota(jnp.int32, (16, 128), 0)
    lane = lax.broadcasted_iota(jnp.int32, (16, 128), 1)
    which = lax.rem(row, 4) * 2 + lane // OBS
    tail = slice(LEAD + 16, LEAD + 32)

    def my_entry(c, head):
        return meta_ref[c, head] - base_ref[0], meta_ref[KEEP + c, head]

    def other_entry(c, head):
        seat = list_ref[c, head].astype(jnp.int32) - base_ref[0]
        return seat, list_ref[KEEP + c, head].astype(jnp.int32)

    def add_score(source, seat, unit, head):
        picked = jnp.where(which == head, tile_ref[source, unit], 0.0).astype(jnp.bfloat16)
        out_ref[seat, tail] = out_ref[seat, tail] + picked

    def put(seat, unit, head):
        cols = slice((head // GROUP) * HD, (head // GROUP + 1) * HD)
        out_ref[seat, :BLOCK] = held_ref[block_rows(unit, 0), cols]
        out_ref[seat, BLOCK:LEAD] = held_ref[block_rows(unit, SHARD), cols]
        add_score(1, seat, unit, head)

    seats(my_entry, functools.partial(add_score, 0))
    seats(other_entry, put)


def pack_far(base, meta, other_pair, mail, got, after):
    return pl.pallas_call(
        far_kernel,
        out_shape=(
            jax.ShapeDtypeStruct((HALF, LEAD + 32, HD), jnp.bfloat16),
            jax.ShapeDtypeStruct((24, 128), jnp.float32),
        ),
        in_specs=[SMEM, SMEM, SMEM, VMEM, VMEM, VMEM] + [ANY] * len(after),
        out_specs=(VMEM, VMEM),
        scratch_shapes=[pltpu.VMEM((2, BLKS, 16, 128), jnp.float32)],
        compiler_params=pltpu.CompilerParams(vmem_limit_bytes=16 * 1024 * 1024),
        cost_estimate=pl.CostEstimate(flops=0, bytes_accessed=3 * 1024 * 1024, transcendentals=0),
        name="pack_far",
    )(base, meta, got[48:56], other_pair, mail, got, *after)


def score_keys(pos, q_ref, k_ref, mail_ref, start):
    rows = [[] for _ in range(1 + BLKS)]
    for kv in range(KVS):
        heads = [
            q_ref[:, (kv * GROUP + g) * HD : (kv * GROUP + g + 1) * HD] for g in range(GROUP)
        ]
        stacked = jnp.concatenate(heads, axis=0)
        score = f32dot(k_ref[:SHARD, kv * HD : (kv + 1) * HD], stacked, NT) * SCALE
        key = lax.broadcasted_iota(jnp.int32, score.shape, 0)
        lane = lax.broadcasted_iota(jnp.int32, score.shape, 1)
        limit = (NSEQ - pos) * SHARD - OBS + lax.rem(lane, OBS)
        score = jnp.where(key <= limit, score, -jnp.inf)
        peak = jnp.max(score, axis=0, keepdims=True)
        expo = jnp.exp(score - peak)
        sums = [
            jnp.sum(expo[b * BLOCK : (b + 1) * BLOCK], axis=0, keepdims=True) for b in range(BLKS)
        ]
        mass = (sums[0] + sums[1]) + (sums[2] + sums[3])
        level = peak + jnp.log(mass)
        for side in range(2):
            cut = slice(side * 128, (side + 1) * 128)
            rows[0].append(level[:, cut])
            for b in range(BLKS):
                rows[1 + b].append((sums[b] / mass)[:, cut])
    for place_, pieces in enumerate(rows):
        at = start + 4 * place_
        mail_ref[at : at + 4] = jnp.concatenate(pieces, axis=0)
    mail_ref[start + 20 : start + 24] = jnp.zeros((4, 128), jnp.float32)


def observe_kernel(pos_ref, q_ref, k_ref, other_ref, meta_ref, *refs):
    mail_ref = refs[-1]
    pos = pos_ref[0]
    score_keys(pos, q_ref, k_ref, mail_ref, 0)
    score_keys(0, q_ref, other_ref, mail_ref, 24)
    mail_ref[48:56] = meta_ref[...].astype(jnp.float32)


def observe(position, observers, keys, other_keys, meta, after):
    return pl.pallas_call(
        observe_kernel,
        out_shape=jax.ShapeDtypeStruct((56, 128), jnp.float32),
        in_specs=[SMEM, VMEM, VMEM, VMEM, VMEM] + [ANY] * len(after),
        out_specs=VMEM,
        compiler_params=pltpu.CompilerParams(vmem_limit_bytes=16 * 1024 * 1024),
        name="observe",
    )(position, observers, keys, other_keys, meta, *after)


def sends(pieces, buf_ref, outs, sems):
    copies = []
    for start, row, count in pieces:
        for side, out_ref in enumerate(outs):
            copies.append(
                pltpu.make_async_copy(
                    buf_ref.at[pl.ds(start, count), side * BLOCK : (side + 1) * BLOCK],
                    out_ref.at[pl.ds(row, count)],
                    sems.at[len(copies)],
                )
            )
    return copies


def place_kernel(half_ref, got_ref, key_ref, value_ref, sems):
    copies = sends(((0, half_ref[0] * HALF, HALF),), got_ref, (key_ref, value_ref), sems)
    for copy in copies:
        copy.start()
    for copy in copies:
        copy.wait()


def place_near(half, got):
    shape = jax.ShapeDtypeStruct((NSEQ, BLOCK, HD), jnp.bfloat16)
    return pl.pallas_call(
        place_kernel,
        out_shape=(shape, shape),
        in_specs=[SMEM, VMEM],
        out_specs=(ANY, ANY),
        scratch_shapes=[pltpu.SemaphoreType.DMA((2,))],
        compiler_params=pltpu.CompilerParams(vmem_limit_bytes=60 * 1024 * 1024),
        cost_estimate=pl.CostEstimate(flops=0, bytes_accessed=4 * 1024 * 1024, transcendentals=0),
        name="place_near",
    )(half, got)


def last_kernel(
    half_ref, got_ref, stats_ref, _k, _v, key_ref, value_ref, recv_ref, block_ref, sems
):
    half, most = half_ref[0], HALF - SHIFT
    other = (1 - half) * HALF
    pieces = (
        (SHIFT * half, other + SHIFT * (1 - half), most),
        (most * (1 - half), other + most * half, SHIFT),
    )
    copies = sends(pieces, got_ref, (key_ref, value_ref), sems)
    for copy in copies:
        copy.start()
    factor = BLKS * NSEQ / OBS
    lead = got_ref[:, LEAD : LEAD + 16].astype(jnp.float32)
    level = (lead[:, 8:12] + lead[:, 4:8]) + lead[:, 0:4]
    top = jnp.max(level, axis=0)
    total = top + jnp.log(jnp.sum(jnp.exp(level - top[None]), axis=0))
    share = jnp.exp(level - total[None])
    tail = got_ref[:, LEAD + 16 :].astype(jnp.float32)
    own = jnp.sum((tail[:, 4:8] + tail[:, 0:4]) * share, axis=1)
    other = jnp.sum((tail[:, 12:16] + tail[:, 8:12]) * share, axis=1)
    low = half_ref[0] == 0
    other = jnp.where(
        low,
        jnp.concatenate([other[HALF - SHIFT :], other[: HALF - SHIFT]], axis=0),
        jnp.concatenate([other[SHIFT:], other[:SHIFT]], axis=0),
    )
    rows = jnp.concatenate(
        [jnp.where(low, own, other), jnp.where(low, other, own)], axis=0
    )
    lined = lax.dot_general(
        jnp.ones((8, 128), jnp.float32),
        rows,
        NT,
        precision=lax.Precision.HIGHEST,
        preferred_element_type=jnp.float32,
    )
    recv_ref[...] = (lined[0:1] * factor).astype(jnp.bfloat16)
    mine = jnp.exp(stats_ref[0:4] - total)
    row = lax.broadcasted_iota(jnp.int32, (HEADS, 4 * 128), 0)
    lane = lax.broadcasted_iota(jnp.int32, (HEADS, 4 * 128), 1)
    chosen = (lane // OBS == row).astype(jnp.float32)
    parts = []
    for b in range(BLKS):
        part = stats_ref[4 + 4 * b : 8 + 4 * b] * mine
        parts.append(jnp.concatenate([part[r : r + 1] for r in range(4)], axis=1))
    table = jnp.concatenate(parts + parts, axis=0)
    scores = lax.dot_general(
        table,
        chosen,
        NT,
        precision=lax.Precision.HIGHEST,
        preferred_element_type=jnp.float32,
    )
    block_ref[...] = scores[:BLKS] * factor
    for copy in copies:
        copy.wait()


def place_last(half, got, stats, earlier):
    shape = jax.ShapeDtypeStruct((NSEQ, BLOCK, HD), jnp.bfloat16)
    return pl.pallas_call(
        last_kernel,
        out_shape=(
            shape,
            shape,
            jax.ShapeDtypeStruct((1, NSEQ), jnp.bfloat16),
            jax.ShapeDtypeStruct((BLKS, HEADS), jnp.float32),
        ),
        in_specs=[SMEM, VMEM, VMEM, ANY, ANY],
        out_specs=(ANY, ANY, VMEM, VMEM),
        scratch_shapes=[pltpu.SemaphoreType.DMA((4,))],
        input_output_aliases={3: 0, 4: 1},
        compiler_params=pltpu.CompilerParams(vmem_limit_bytes=16 * 1024 * 1024),
        cost_estimate=pl.CostEstimate(flops=0, bytes_accessed=4 * 1024 * 1024, transcendentals=0),
        name="place_last",
    )(half, got, stats, *earlier)


def at(zh, y, x, c):
    return ((zh * 4 + y) * 4 + x) * 2 + c


def spread(tail):
    me = lax.axis_index(SEQ)
    held = jnp.where(me == NSEQ - 1, tail, jnp.zeros_like(tail))
    four = range(4)
    steps = (
        [[(at(1, 3, 3, 1), at(1, y, 3, 1))] for y in range(3)],
        [[(at(1, y, 3, 1), at(1, y, x, 1)) for y in four] for x in range(3)],
        [[(at(1, y, x, 1), at(1, y, x, 0)) for y in four for x in four]],
    )
    levels = []
    for step in steps:
        came = [lax.ppermute(held, SEQ, pairs) for pairs in step]
        for part in came:
            held = held + part
        levels.append(held)
    return levels


def shards(queries, keys, values, kept_index, kept_count, owner):
    position = lax.axis_index(SEQ)
    zh = lax.axis_index("zh")
    pos = position.reshape(1).astype(jnp.int32)
    near_half = zh.reshape(1).astype(jnp.int32)
    base = near_half * HALF
    slot_ids = jnp.arange(KEEP, dtype=jnp.int32)[:, None]
    owners = jnp.transpose(owner, (0, 2, 1))[0]
    picks = jnp.transpose(kept_index, (0, 2, 1))[0]
    meta = jnp.concatenate([jnp.where(slot_ids < kept_count, owners, -1), picks], axis=0)
    meta = jnp.pad(meta, ((0, 0), (0, 128 - HEADS)))

    def exchange(packed):
        return lax.all_to_all(packed, PLANE, split_axis=0, concat_axis=0, tiled=True)

    def hop(pair, by):
        steps = [(i, i + by) for i in range(NSEQ) if i // HALF == (i + by) // HALF]
        return lax.ppermute(pair, SEQ, steps)

    swap = []
    for i in range(HALF):
        j = HALF + (i + SHIFT) % HALF
        swap += [(i, j), (j, i)]
    levels = spread(queries[SHARD - OBS :])
    pair = join(keys, values)
    other_pair = lax.ppermute(pair, SEQ, swap)
    one, two = hop(pair, 1), hop(pair, 2)
    three = hop(two, 1)
    edge_a = lax.ppermute(other_pair, SEQ, [(32, 33), (33, 32)])
    edge_b = lax.ppermute(other_pair, SEQ, [(33, 34), (63, 32)])

    near = exchange(pack_near(base, meta, pair, (other_pair, one, two, three, levels[2], edge_a, edge_b)))
    mail = observe(pos, levels[-1], pair, other_pair, meta, ())
    got = lax.ppermute(mail, SEQ, swap)
    packed, stats = pack_far(base, meta, other_pair, mail, got, ())
    far = exchange(packed)
    attended = attend(pos, queries, [pair, one, two, three, other_pair, edge_a, edge_b])
    first = place_near(near_half, near)
    recv_keys, recv_values, recv_scores, scores_here = place_last(near_half, far, stats, first)
    return (
        attended,
        scores_here.T,
        recv_keys.reshape(1, 1, NSEQ, 1, BLOCK, HD),
        recv_values.reshape(1, 1, NSEQ, 1, BLOCK, HD),
        recv_scores.reshape(1, 1, NSEQ, 1),
    )


def solution(mesh):
    fine = Mesh(mesh.devices.reshape(2, 4, 4, 2, 4), SEQ + ("kv",))
    placed = (
        P(SEQ, "kv"),
        P(SEQ, "kv"),
        P(SEQ, "kv"),
        P(SEQ, "kv", None),
        P(SEQ, "kv"),
        P(SEQ, "kv", None),
    )
    return jax.shard_map(
        shards,
        mesh=fine,
        in_specs=placed,
        out_specs=(
            P(SEQ, "kv"),
            P("kv", SEQ),
            P(SEQ, "kv", None, None, None, None),
            P(SEQ, "kv", None, None, None, None),
            P(SEQ, "kv", None, None),
        ),
        check_vma=False,
    )
```

```python
import functools
import math

import jax
import jax.numpy as jnp
from jax import lax
from jax.experimental import pallas as pl
from jax.experimental.pallas import tpu as pltpu
from jax.sharding import Mesh, PartitionSpec as P

HD = 128
CYCLE = 4
OBS = 64
BLOCK = 128
SHARD = 512
HEADS = 8
KVS = 2
GROUP = 4
KEEP = 4
BLKS = 4
NSEQ = 64
HALF = 32
SEQ = ("zh", "y", "x", "c")
PLANE = ("y", "x", "c")
PAIRS = 7
LEAD = 2 * BLOCK
SHIFT = 2
LOG2E = 1.4426950408889634
COEF = LOG2E / math.sqrt(HD)
SCALE = 1.0 / math.sqrt(HD)
BIG = 1e30
NT = (((1,), (1,)), ((), ()))
NN = (((1,), (0,)), ((), ()))


def f32dot(a, b, dims):
    return lax.dot_general(a, b, dims, preferred_element_type=jnp.float32)


def attend_kernel(pos_ref, q_from, *refs):
    o_ref, q_all, held_all, sems = refs[-4:]
    pos = pos_ref[0]
    head = pl.program_id(0)

    @pl.when(head == 0)
    def _():
        copies = [pltpu.make_async_copy(q_from, q_all, sems.at[PAIRS])]
        for i in range(PAIRS):
            copies.append(pltpu.make_async_copy(refs[i], held_all.at[i], sems.at[i]))
        for copy in copies:
            copy.start()
        for copy in copies:
            copy.wait()

    cols = pl.ds(pl.multiple_of((head // GROUP) * HD, HD), HD)
    sides = (slice(0, SHARD), slice(SHARD, 2 * SHARD))
    p0, p1, p2, p3, held, ea, eb = [
        [held_all.at[i, side, cols] for side in sides] for i in range(PAIRS)
    ]
    q_ref = q_all.at[:, pl.ds(pl.multiple_of(head * HD, HD), HD)]
    first = pos - NSEQ // 2
    keys, values = [p0[0][...]], [p0[1][...]]
    for side, out in ((0, keys), (1, values)):
        near = [p[side][...] for p in (p1, p2, p3)]
        other, swapped, edge = [e[side][...] for e in (held, ea, eb)]
        out.append(jnp.where(first == 0, swapped, near[0]))
        out.append(jnp.where((first == 0) | (first == 1), other, near[1]))
        third = jnp.where((first == 0) | (first == 2), edge, near[2])
        out.append(jnp.where(first == 1, swapped, third))
    half = SHARD // 2
    ones = jnp.ones((SHARD, HD), jnp.bfloat16)
    vext = [jnp.concatenate([v, ones], axis=1) for v in values]
    row = lax.broadcasted_iota(jnp.int32, (half, half), 0)
    col = lax.broadcasted_iota(jnp.int32, (half, half), 1)
    causal = col <= row
    for tile in range(2):
        q = q_ref[tile * half : (tile + 1) * half, :]
        diag = f32dot(q, keys[0][tile * half : (tile + 1) * half, :], NT)
        diag = jnp.where(causal, diag, -BIG)
        peak = jnp.max(diag, axis=1, keepdims=True)
        if tile == 1:
            own = f32dot(q, keys[0][:half, :], NT)
            peak = jnp.maximum(peak, jnp.max(own, axis=1, keepdims=True))
        past = [f32dot(q, k, NT) for k in keys[1:]]
        for distance, score in enumerate(past, 1):
            here = jnp.max(score, axis=1, keepdims=True)
            peak = jnp.where(pos >= distance, jnp.maximum(peak, here), peak)
        shift = peak * COEF
        weight = jnp.exp2(diag * COEF - shift).astype(jnp.bfloat16)
        acc = f32dot(weight, vext[0][tile * half : (tile + 1) * half], NN)
        if tile == 1:
            weight = jnp.exp2(own * COEF - shift).astype(jnp.bfloat16)
            acc += f32dot(weight, vext[0][:half], NN)
        for distance, score in enumerate(past, 1):
            lift = jnp.where(pos >= distance, shift, BIG)
            weight = jnp.exp2(score * COEF - lift).astype(jnp.bfloat16)
            acc += f32dot(weight, vext[distance], NN)
        mixed = acc[:, :HD] / acc[:, HD:]
        o_ref[tile * half : (tile + 1) * half, :] = mixed.astype(jnp.bfloat16)


def attend(position, queries, pairs):
    return pl.pallas_call(
        attend_kernel,
        grid=(HEADS,),
        out_shape=jax.ShapeDtypeStruct((SHARD, HEADS * HD), jnp.bfloat16),
        in_specs=[pl.BlockSpec(memory_space=pltpu.SMEM)]
        + [pl.BlockSpec(memory_space=pl.ANY)] * (1 + PAIRS),
        out_specs=pl.BlockSpec((SHARD, HD), lambda h: (0, h)),
        scratch_shapes=[
            pltpu.VMEM((SHARD, HEADS * HD), jnp.bfloat16),
            pltpu.VMEM((PAIRS, 2 * SHARD, KVS * HD), jnp.bfloat16),
            pltpu.SemaphoreType.DMA((PAIRS + 1,)),
        ],
        compiler_params=pltpu.CompilerParams(vmem_limit_bytes=60 * 1024 * 1024),
        cost_estimate=pl.CostEstimate(
            flops=HEADS * SHARD * SHARD * 4 * HD * 4,
            bytes_accessed=4 * 1024 * 1024,
            transcendentals=HEADS * SHARD * SHARD * 4,
        ),
        name="attend",
    )(position, queries, *pairs)


SMEM = pl.BlockSpec(memory_space=pltpu.SMEM)
VMEM = pl.BlockSpec(memory_space=pltpu.VMEM)
ANY = pl.BlockSpec(memory_space=pl.ANY)


def join_kernel(k_ref, v_ref, pair_ref, sems):
    copies = (
        pltpu.make_async_copy(k_ref, pair_ref.at[:SHARD], sems.at[0]),
        pltpu.make_async_copy(v_ref, pair_ref.at[SHARD:], sems.at[1]),
    )
    for copy in copies:
        copy.start()
    for copy in copies:
        copy.wait()


def join(keys, values):
    return pl.pallas_call(
        join_kernel,
        out_shape=jax.ShapeDtypeStruct((2 * SHARD, KVS * HD), jnp.bfloat16),
        in_specs=[ANY, ANY],
        out_specs=VMEM,
        scratch_shapes=[pltpu.SemaphoreType.DMA((2,))],
        cost_estimate=pl.CostEstimate(flops=0, bytes_accessed=1024 * 1024, transcendentals=0),
        name="join",
    )(keys, values)


def seats(entry, put):
    for head in range(HEADS):
        for c in range(KEEP):
            seat, unit = entry(c, head)
            pl.when((seat >= 0) & (seat < HALF))(functools.partial(put, seat, unit, head))


def block_rows(unit, start):
    return pl.ds(pl.multiple_of(unit * BLOCK + start, BLOCK), BLOCK)


def near_kernel(base_ref, meta_ref, pair_ref, *refs):
    out_ref = refs[-1]
    out_ref[...] = jnp.zeros_like(out_ref)

    def entry(c, head):
        return meta_ref[c, head] - base_ref[0], meta_ref[KEEP + c, head]

    def put(seat, unit, head):
        cols = slice((head // GROUP) * HD, (head // GROUP + 1) * HD)
        out_ref[seat, :BLOCK] = pair_ref[block_rows(unit, 0), cols]
        out_ref[seat, BLOCK:] = pair_ref[block_rows(unit, SHARD), cols]

    seats(entry, put)


def pack_near(base, meta, pair, after):
    return pl.pallas_call(
        near_kernel,
        out_shape=jax.ShapeDtypeStruct((HALF, 2 * BLOCK, HD), jnp.bfloat16),
        in_specs=[SMEM, SMEM, VMEM] + [ANY] * len(after),
        out_specs=VMEM,
        compiler_params=pltpu.CompilerParams(vmem_limit_bytes=60 * 1024 * 1024),
        cost_estimate=pl.CostEstimate(flops=0, bytes_accessed=3 * 1024 * 1024, transcendentals=0),
        name="pack_near",
    )(base, meta, pair, *after)


def terms(value, count):
    parts = []
    for _ in range(count):
        part = value.astype(jnp.bfloat16)
        parts.append(part)
        value = value - part.astype(jnp.float32)
    return parts


def far_kernel(base_ref, meta_ref, list_ref, held_ref, mail_ref, got_ref, *refs):
    out_ref, stats_ref, tile_ref = refs[-3:]
    last = base_ref[0] > 0
    mine = jnp.where(last, mail_ref[0:24], got_ref[24:48])
    other = jnp.where(last, mail_ref[24:48], got_ref[0:24])
    stats_ref[...] = mine
    level, other_level = mine[0:4], other[0:4]
    top = jnp.maximum(level, other_level)
    both = top + jnp.log(jnp.exp(level - top) + jnp.exp(other_level - top))
    part, other_part = jnp.exp(level - both), jnp.exp(other_level - both)
    blank = jnp.zeros((4, 128), jnp.float32)
    as_rows = lambda pieces: jnp.concatenate([p.astype(jnp.float32) for p in pieces], axis=0)
    for b in range(BLKS):
        rows = slice(4 + 4 * b, 8 + 4 * b)
        tile_ref[0, b] = as_rows(terms(mine[rows] * part, 2) + [blank, blank])
        tile_ref[1, b] = as_rows([blank, blank] + terms(other[rows] * other_part, 2))
    out_ref[:, :LEAD, :] = jnp.zeros((HALF, LEAD, HD), jnp.bfloat16)
    lead = as_rows(terms(both, 3) + [blank]).astype(jnp.bfloat16)
    out_ref[:, LEAD : LEAD + 16, :] = jnp.broadcast_to(lead[None], (HALF, 16, HD))
    out_ref[:, LEAD + 16 :, :] = jnp.zeros((HALF, 16, HD), jnp.bfloat16)
    row = lax.broadcasted_iota(jnp.int32, (16, 128), 0)
    lane = lax.broadcasted_iota(jnp.int32, (16, 128), 1)
    which = lax.rem(row, 4) * 2 + lane // OBS
    tail = slice(LEAD + 16, LEAD + 32)

    def my_entry(c, head):
        return meta_ref[c, head] - base_ref[0], meta_ref[KEEP + c, head]

    def other_entry(c, head):
        seat = list_ref[c, head].astype(jnp.int32) - base_ref[0]
        return seat, list_ref[KEEP + c, head].astype(jnp.int32)

    def add_score(source, seat, unit, head):
        picked = jnp.where(which == head, tile_ref[source, unit], 0.0).astype(jnp.bfloat16)
        out_ref[seat, tail] = out_ref[seat, tail] + picked

    def put(seat, unit, head):
        cols = slice((head // GROUP) * HD, (head // GROUP + 1) * HD)
        out_ref[seat, :BLOCK] = held_ref[block_rows(unit, 0), cols]
        out_ref[seat, BLOCK:LEAD] = held_ref[block_rows(unit, SHARD), cols]
        add_score(1, seat, unit, head)

    seats(my_entry, functools.partial(add_score, 0))
    seats(other_entry, put)


def pack_far(base, meta, other_pair, mail, got, after):
    return pl.pallas_call(
        far_kernel,
        out_shape=(
            jax.ShapeDtypeStruct((HALF, LEAD + 32, HD), jnp.bfloat16),
            jax.ShapeDtypeStruct((24, 128), jnp.float32),
        ),
        in_specs=[SMEM, SMEM, SMEM, VMEM, VMEM, VMEM] + [ANY] * len(after),
        out_specs=(VMEM, VMEM),
        scratch_shapes=[pltpu.VMEM((2, BLKS, 16, 128), jnp.float32)],
        compiler_params=pltpu.CompilerParams(vmem_limit_bytes=16 * 1024 * 1024),
        cost_estimate=pl.CostEstimate(flops=0, bytes_accessed=3 * 1024 * 1024, transcendentals=0),
        name="pack_far",
    )(base, meta, got[48:56], other_pair, mail, got, *after)


def score_keys(pos, q_ref, k_ref, mail_ref, start):
    rows = [[] for _ in range(1 + BLKS)]
    for kv in range(KVS):
        heads = [
            q_ref[:, (kv * GROUP + g) * HD : (kv * GROUP + g + 1) * HD] for g in range(GROUP)
        ]
        stacked = jnp.concatenate(heads, axis=0)
        score = f32dot(k_ref[:SHARD, kv * HD : (kv + 1) * HD], stacked, NT) * SCALE
        key = lax.broadcasted_iota(jnp.int32, score.shape, 0)
        lane = lax.broadcasted_iota(jnp.int32, score.shape, 1)
        limit = (NSEQ - pos) * SHARD - OBS + lax.rem(lane, OBS)
        score = jnp.where(key <= limit, score, -jnp.inf)
        peak = jnp.max(score, axis=0, keepdims=True)
        expo = jnp.exp(score - peak)
        sums = [
            jnp.sum(expo[b * BLOCK : (b + 1) * BLOCK], axis=0, keepdims=True) for b in range(BLKS)
        ]
        mass = (sums[0] + sums[1]) + (sums[2] + sums[3])
        level = peak + jnp.log(mass)
        for side in range(2):
            cut = slice(side * 128, (side + 1) * 128)
            rows[0].append(level[:, cut])
            for b in range(BLKS):
                rows[1 + b].append((sums[b] / mass)[:, cut])
    for place_, pieces in enumerate(rows):
        at = start + 4 * place_
        mail_ref[at : at + 4] = jnp.concatenate(pieces, axis=0)
    mail_ref[start + 20 : start + 24] = jnp.zeros((4, 128), jnp.float32)


def observe_kernel(pos_ref, q_ref, k_ref, other_ref, meta_ref, *refs):
    mail_ref = refs[-1]
    pos = pos_ref[0]
    score_keys(pos, q_ref, k_ref, mail_ref, 0)
    score_keys(0, q_ref, other_ref, mail_ref, 24)
    mail_ref[48:56] = meta_ref[...].astype(jnp.float32)


def observe(position, observers, keys, other_keys, meta, after):
    return pl.pallas_call(
        observe_kernel,
        out_shape=jax.ShapeDtypeStruct((56, 128), jnp.float32),
        in_specs=[SMEM, VMEM, VMEM, VMEM, VMEM] + [ANY] * len(after),
        out_specs=VMEM,
        compiler_params=pltpu.CompilerParams(vmem_limit_bytes=16 * 1024 * 1024),
        name="observe",
    )(position, observers, keys, other_keys, meta, *after)


def sends(pieces, buf_ref, outs, sems):
    copies = []
    for start, row, count in pieces:
        for side, out_ref in enumerate(outs):
            copies.append(
                pltpu.make_async_copy(
                    buf_ref.at[pl.ds(start, count), side * BLOCK : (side + 1) * BLOCK],
                    out_ref.at[pl.ds(row, count)],
                    sems.at[len(copies)],
                )
            )
    return copies


def place_kernel(half_ref, got_ref, key_ref, value_ref, sems):
    copies = sends(((0, half_ref[0] * HALF, HALF),), got_ref, (key_ref, value_ref), sems)
    for copy in copies:
        copy.start()
    for copy in copies:
        copy.wait()


def place_near(half, got):
    shape = jax.ShapeDtypeStruct((NSEQ, BLOCK, HD), jnp.bfloat16)
    return pl.pallas_call(
        place_kernel,
        out_shape=(shape, shape),
        in_specs=[SMEM, VMEM],
        out_specs=(ANY, ANY),
        scratch_shapes=[pltpu.SemaphoreType.DMA((2,))],
        compiler_params=pltpu.CompilerParams(vmem_limit_bytes=60 * 1024 * 1024),
        cost_estimate=pl.CostEstimate(flops=0, bytes_accessed=4 * 1024 * 1024, transcendentals=0),
        name="place_near",
    )(half, got)


def last_kernel(
    half_ref, got_ref, stats_ref, _k, _v, key_ref, value_ref, recv_ref, block_ref, sems
):
    half, most = half_ref[0], HALF - SHIFT
    other = (1 - half) * HALF
    pieces = (
        (SHIFT * half, other + SHIFT * (1 - half), most),
        (most * (1 - half), other + most * half, SHIFT),
    )
    copies = sends(pieces, got_ref, (key_ref, value_ref), sems)
    for copy in copies:
        copy.start()
    factor = BLKS * NSEQ / OBS
    lead = got_ref[:, LEAD : LEAD + 16].astype(jnp.float32)
    level = (lead[:, 8:12] + lead[:, 4:8]) + lead[:, 0:4]
    top = jnp.max(level, axis=0)
    total = top + jnp.log(jnp.sum(jnp.exp(level - top[None]), axis=0))
    share = jnp.exp(level - total[None])
    tail = got_ref[:, LEAD + 16 :].astype(jnp.float32)
    own = jnp.sum((tail[:, 4:8] + tail[:, 0:4]) * share, axis=1)
    other = jnp.sum((tail[:, 12:16] + tail[:, 8:12]) * share, axis=1)
    low = half_ref[0] == 0
    other = jnp.where(
        low,
        jnp.concatenate([other[HALF - SHIFT :], other[: HALF - SHIFT]], axis=0),
        jnp.concatenate([other[SHIFT:], other[:SHIFT]], axis=0),
    )
    rows = jnp.concatenate(
        [jnp.where(low, own, other), jnp.where(low, other, own)], axis=0
    )
    lined = lax.dot_general(
        jnp.ones((8, 128), jnp.float32),
        rows,
        NT,
        precision=lax.Precision.HIGHEST,
        preferred_element_type=jnp.float32,
    )
    recv_ref[...] = (lined[0:1] * factor).astype(jnp.bfloat16)
    mine = jnp.exp(stats_ref[0:4] - total)
    row = lax.broadcasted_iota(jnp.int32, (HEADS, 4 * 128), 0)
    lane = lax.broadcasted_iota(jnp.int32, (HEADS, 4 * 128), 1)
    chosen = (lane // OBS == row).astype(jnp.float32)
    parts = []
    for b in range(BLKS):
        part = stats_ref[4 + 4 * b : 8 + 4 * b] * mine
        parts.append(jnp.concatenate([part[r : r + 1] for r in range(4)], axis=1))
    table = jnp.concatenate(parts + parts, axis=0)
    scores = lax.dot_general(
        table,
        chosen,
        NT,
        precision=lax.Precision.HIGHEST,
        preferred_element_type=jnp.float32,
    )
    block_ref[...] = scores[:BLKS] * factor
    for copy in copies:
        copy.wait()


def place_last(half, got, stats, earlier):
    shape = jax.ShapeDtypeStruct((NSEQ, BLOCK, HD), jnp.bfloat16)
    return pl.pallas_call(
        last_kernel,
        out_shape=(
            shape,
            shape,
            jax.ShapeDtypeStruct((1, NSEQ), jnp.bfloat16),
            jax.ShapeDtypeStruct((BLKS, HEADS), jnp.float32),
        ),
        in_specs=[SMEM, VMEM, VMEM, ANY, ANY],
        out_specs=(ANY, ANY, VMEM, VMEM),
        scratch_shapes=[pltpu.SemaphoreType.DMA((4,))],
        input_output_aliases={3: 0, 4: 1},
        compiler_params=pltpu.CompilerParams(vmem_limit_bytes=16 * 1024 * 1024),
        cost_estimate=pl.CostEstimate(flops=0, bytes_accessed=4 * 1024 * 1024, transcendentals=0),
        name="place_last",
    )(half, got, stats, *earlier)


def at(zh, y, x, c):
    return ((zh * 4 + y) * 4 + x) * 2 + c


def spread(tail):
    me = lax.axis_index(SEQ)
    held = jnp.where(me == NSEQ - 1, tail, jnp.zeros_like(tail))
    four = range(4)
    steps = (
        [[(at(1, 3, 3, 1), at(1, y, 3, 1))] for y in range(3)],
        [[(at(1, y, 3, 1), at(1, y, x, 1)) for y in four] for x in range(3)],
        [[(at(1, y, x, 1), at(1, y, x, 0)) for y in four for x in four]],
    )
    levels = []
    for step in steps:
        came = [lax.ppermute(held, SEQ, pairs) for pairs in step]
        for part in came:
            held = held + part
        levels.append(held)
    return levels


def shards(queries, keys, values, kept_index, kept_count, owner):
    position = lax.axis_index(SEQ)
    zh = lax.axis_index("zh")
    pos = position.reshape(1).astype(jnp.int32)
    near_half = zh.reshape(1).astype(jnp.int32)
    base = near_half * HALF
    slot_ids = jnp.arange(KEEP, dtype=jnp.int32)[:, None]
    owners = jnp.transpose(owner, (0, 2, 1))[0]
    picks = jnp.transpose(kept_index, (0, 2, 1))[0]
    meta = jnp.concatenate([jnp.where(slot_ids < kept_count, owners, -1), picks], axis=0)
    meta = jnp.pad(meta, ((0, 0), (0, 128 - HEADS)))

    def exchange(packed):
        return lax.all_to_all(packed, PLANE, split_axis=0, concat_axis=0, tiled=True)

    def hop(pair, by):
        steps = [(i, i + by) for i in range(NSEQ) if i // HALF == (i + by) // HALF]
        return lax.ppermute(pair, SEQ, steps)

    swap = []
    for i in range(HALF):
        j = HALF + (i + SHIFT) % HALF
        swap += [(i, j), (j, i)]
    levels = spread(queries[SHARD - OBS :])
    pair = join(keys, values)
    other_pair = lax.ppermute(pair, SEQ, swap)
    one, two = hop(pair, 1), hop(pair, 2)
    three = hop(two, 1)
    edge_a = lax.ppermute(other_pair, SEQ, [(32, 33), (33, 32)])
    edge_b = lax.ppermute(other_pair, SEQ, [(33, 34), (63, 32)])

    near = exchange(pack_near(base, meta, pair, (one, three, levels[2], edge_a, edge_b)))
    mail = observe(pos, levels[-1], pair, other_pair, meta, ())
    got = lax.ppermute(mail, SEQ, swap)
    packed, stats = pack_far(base, meta, other_pair, mail, got, ())
    far = exchange(packed)
    attended = attend(pos, queries, [pair, one, two, three, other_pair, edge_a, edge_b])
    first = place_near(near_half, near)
    recv_keys, recv_values, recv_scores, scores_here = place_last(near_half, far, stats, first)
    return (
        attended,
        scores_here.T,
        recv_keys.reshape(1, 1, NSEQ, 1, BLOCK, HD),
        recv_values.reshape(1, 1, NSEQ, 1, BLOCK, HD),
        recv_scores.reshape(1, 1, NSEQ, 1),
    )


def solution(mesh):
    fine = Mesh(mesh.devices.reshape(2, 4, 4, 2, 4), SEQ + ("kv",))
    placed = (
        P(SEQ, "kv"),
        P(SEQ, "kv"),
        P(SEQ, "kv"),
        P(SEQ, "kv", None),
        P(SEQ, "kv"),
        P(SEQ, "kv", None),
    )
    return jax.shard_map(
        shards,
        mesh=fine,
        in_specs=placed,
        out_specs=(
            P(SEQ, "kv"),
            P("kv", SEQ),
            P(SEQ, "kv", None, None, None, None),
            P(SEQ, "kv", None, None, None, None),
            P(SEQ, "kv", None, None),
        ),
        check_vma=False,
    )
```
